512 devices in a mesh: leaf: 16 (over x_lo, z), prow: 8 (over y), pcol: 4 (over x_hi, core).
Axes of the slice: x: 4 (x_hi: 2, x_lo: 2; x = x_hi * 2 + x_lo), y: 8, z: 8, core: 2. Of those that a mesh axis runs over, the one named last changes fastest.
Arguments:
- ancestor_inverse: float32 [6144, 6144], P(('prow', 'pcol'), 'leaf'), as said below
- pattern: int32 [16, 8], P('leaf'), may hold values from 0 to 47, as said below
- child_lower: float32 [16, 1024, 896], P('leaf', ('prow', 'pcol')), may hold values from -0.1875 to 0.1875
- child_diag_inv: float32 [16, 896, 896], P('leaf', ('prow', 'pcol')), as said below
Outputs:
- cross_inverse: float32 [16, 6144, 896], P('leaf', ('prow', 'pcol'))
- diag_inverse: float32 [16, 896, 896], P('leaf', ('prow', 'pcol'))
The draws below stay inside these ranges and needn't reach their ends.
Inputs may be any that keep to these rules, and one draw needn't show every extreme that they name: `pattern`: each row holds 8 different root block numbers in increasing order. `ancestor_inverse`: symmetric. `child_diag_inv`: symmetric in its last two dimensions.
All inputs are finite; a program needn't handle non-finite values.
Results may differ from the reference program's by a relative error of at most 0.0003.
Values sent between devices are 32-bit elements; how exact they have to be, the bound alone decides.
No kernel may reach another device: no remote copies, remote signals or barrier semaphores. Data moves between devices by JAX's collectives and lax.ppermute only.
A program may use at most 128 MiB of HBM per device.

```python
import jax
import jax.numpy as jnp
from jax import lax

BLK = 128
S0 = 6144
S1 = 896
NP = 8
N_LEAF = 16


def draw_pattern(key, part):
    key = jax.random.fold_in(key, 1)
    child_keys = jax.random.split(key, N_LEAF)
    shuffled = jax.vmap(lambda child_key: jax.random.permutation(child_key, S0 // BLK))(child_keys)
    return jnp.sort(shuffled[:, :NP], axis=1).astype(jnp.int32)


def draw_ancestor_inverse(key, part):
    key = jax.random.fold_in(key, 2)
    first_key, second_key = jax.random.split(key, 2)
    gaussian = jax.random.normal(first_key, (S0, S0), jnp.float32)
    symmetric = (gaussian + gaussian.T) * (0.5 / S0 ** 0.5)
    diagonal = jax.random.uniform(second_key, (S0,), jnp.float32, 1.0, 2.0)
    symmetric = symmetric + jnp.diag(diagonal)
    return symmetric


def draw_child_diag_inv(key, part):
    key = jax.random.fold_in(key, 3)
    first_key, second_key = jax.random.split(key, 2)
    gaussian = jax.random.normal(first_key, (N_LEAF, S1, S1), jnp.float32)
    symmetric = (gaussian + jnp.swapaxes(gaussian, 1, 2)) * (0.5 / S1 ** 0.5)
    diagonal = jax.random.uniform(second_key, (N_LEAF, S1), jnp.float32, 1.0, 2.0)
    symmetric = symmetric + diagonal[:, :, None] * jnp.eye(S1, dtype=jnp.float32)[None]
    return symmetric


def steps_of(rng, dims, pieces, low, largest):
    level, own = 1.0, jax.random.fold_in(rng, 6)
    for axis_at, blocks in pieces:
        draws = jnp.exp(jax.random.uniform(jax.random.fold_in(own, axis_at), (blocks,), jnp.float32, low / len(pieces), largest / len(pieces)))
        level = level * jnp.repeat(draws, dims[axis_at] // blocks).reshape([-1 if axis == axis_at else 1 for axis in range(len(dims))])
    return level


def scatter_about(rng, dims, scale, limit, cuts=(), kind=jnp.bfloat16):
    array = scale * jax.random.normal(rng, dims, jnp.float32)
    if cuts:
        array = array * steps_of(rng, dims, cuts, -0.22, 0.18)
    return jnp.clip(array, -limit, limit).astype(kind)


def setup_inputs(seed: int = 0) -> dict:
    key_list = jax.random.split(jax.random.key(seed), 5)
    return {
        "ancestor_inverse": draw_ancestor_inverse(jax.random.fold_in(key_list[4], 71), 0),
        "pattern": draw_pattern(jax.random.fold_in(key_list[4], 71), 0),
        "child_lower": scatter_about(key_list[2], (N_LEAF, NP * BLK, S1), (NP * BLK) ** -0.5, 0.1875, ((0, 16), (1, 32)), jnp.float32),
        "child_diag_inv": draw_child_diag_inv(jax.random.fold_in(key_list[4], 71), 0),
    }


highest = lax.Precision.HIGHEST


def reference(ancestor_inverse, pattern, child_lower, child_diag_inv):
    offsets = jnp.arange(BLK, dtype=jnp.int32)

    def one_child(packed):
        pattern_row, lower_rows, diag_inv = packed
        root_rows = (pattern_row[:, None].astype(jnp.int32) * BLK + offsets[None, :]).reshape(-1)
        columns = jnp.take(ancestor_inverse, root_rows, axis=1)
        product = jnp.dot(columns, lower_rows, precision=highest, preferred_element_type=jnp.float32)
        picked = jnp.take(product, root_rows, axis=0)
        diagonal = diag_inv + jnp.dot(lower_rows.T, picked, precision=highest, preferred_element_type=jnp.float32)
        return -product, diagonal

    cross_block, diagonal = lax.map(one_child, (pattern, child_lower, child_diag_inv))
    return cross_block, diagonal
```

```python
import jax
import jax.numpy as jnp
from jax import lax
from jax.experimental import pallas as pl
from jax.experimental.pallas import tpu as pltpu
from jax.sharding import PartitionSpec as P

BLK = 128
NP = 8
N_LEAF = 16
N_GRID = 32
ROWS = 192
CHUNK = ROWS // N_LEAF
OWN_BLOCKS = 3
S1 = 896
COLS = S1 // N_GRID
LROWS = 32
PAT_ROW = OWN_BLOCKS * CHUNK
PIECE1 = 40
PIECE2 = NP * CHUNK
PIECE3 = 48
HALF_ROW = 32
VMEM_LIMIT = 48 * 1024 * 1024


def in_vmem(count):
    return [pl.BlockSpec(memory_space=pltpu.VMEM)] * count


def split(value):
    high = value.astype(jnp.bfloat16)
    low = (value - high.astype(jnp.float32)).astype(jnp.bfloat16)
    return high, low


def spread_kernel(ancestor, pattern, out):
    row = pattern[...].astype(jnp.float32)
    for leaf in range(N_LEAF):
        for block in range(OWN_BLOCKS):
            out[leaf, block * CHUNK:(block + 1) * CHUNK, :] = ancestor[
                leaf * CHUNK:(leaf + 1) * CHUNK, block * BLK:(block + 1) * BLK
            ]
        out[leaf, PAT_ROW:PIECE1, :] = jnp.zeros((PIECE1 - PAT_ROW, BLK), jnp.float32)
        out[leaf, PAT_ROW:PAT_ROW + 1, 0:NP] = row


def select_kernel(pieces, out, patterns, semaphore):
    copy = pltpu.make_async_copy(pieces.at[:, PAT_ROW:PAT_ROW + 1, :], patterns, semaphore)
    copy.start()
    copy.wait()

    def one_leaf(leaf, carry):
        for block in range(NP):
            number = patterns[leaf, 0, block].astype(jnp.int32)
            owner = number // OWN_BLOCKS
            first = (number - owner * OWN_BLOCKS) * CHUNK
            out[leaf, block * CHUNK:(block + 1) * CHUNK, :] = pieces[owner, pl.ds(first, CHUNK), :]
        return carry

    lax.fori_loop(0, N_LEAF, one_leaf, 0)


def cross_kernel(pieces, own, other, cross, out, lower_high, lower_low, panel, product):
    column = lax.axis_index("pcol")
    core = lax.rem(column, 2)
    side = column // 2
    for source, at_core in ((own, core), (other, 1 - core)):
        for block in range(NP):
            for part, at_side in ((0, side), (1, 1 - side)):
                high, low = split(source[block, part * LROWS:(part + 1) * LROWS, :])
                first = pl.multiple_of(block * BLK + at_side * 64 + at_core * LROWS, LROWS)
                lower_high[pl.ds(first, LROWS), :] = high
                lower_low[pl.ds(first, LROWS), :] = low
    for leaf in range(N_LEAF):
        for block in range(NP):
            panel[leaf * CHUNK:(leaf + 1) * CHUNK, block * BLK:(block + 1) * BLK] = pieces[
                leaf, block * CHUNK:(block + 1) * CHUNK, :
            ]
    panel_high, panel_low = split(panel[...])

    def dot(a, b):
        return jnp.dot(a, b, preferred_element_type=jnp.float32)

    value = dot(panel_high, lower_high[...]) + (
        dot(panel_low, lower_high[...]) + dot(panel_high, lower_low[...])
    )
    product[...] = value
    cross[0, :, :] = -value
    whole = product[pl.ds(pl.multiple_of(core * 64, 64), BLK), :].T
    half = product[pl.ds(pl.multiple_of((1 - core) * BLK, BLK), 64), :].T
    for device in range(N_GRID):
        at = device * COLS
        out[device, 0:COLS, :] = whole[at:at + COLS, :]
        out[device, HALF_ROW:HALF_ROW + COLS // 2, 0:64] = half[at:at + COLS // 2, :]
        out[device, HALF_ROW:HALF_ROW + COLS // 2, 64:128] = half[at + COLS // 2:at + COLS, :]


def diagonal_kernel(pattern, pieces, lower_high, lower_low, child, out, rows):
    lane = lax.broadcasted_iota(jnp.int32, (COLS // 2, BLK), 1)
    for block in range(NP):
        number = pattern[0, block]
        group = number // 3
        place = number - group * 3
        upper = 2 * group
        middle = place == 1
        whole = pieces[upper + place // 2, 0:COLS, :]
        first = pieces[upper, HALF_ROW:HALF_ROW + COLS // 2, :]
        second = pieces[upper + 1, HALF_ROW:HALF_ROW + COLS // 2, :]
        top = jnp.where(lane < 64, first, pltpu.roll(second, 64, 1))
        bottom = jnp.where(lane < 64, pltpu.roll(first, 64, 1), second)
        here = slice(block * BLK, (block + 1) * BLK)
        rows[0:COLS // 2, here] = jnp.where(middle, top, whole[0:COLS // 2, :])
        rows[COLS // 2:COLS, here] = jnp.where(middle, bottom, whole[COLS // 2:COLS, :])
    rows[COLS:, :] = jnp.zeros((32 - COLS, NP * BLK), jnp.float32)
    high, low = split(rows[...])

    def dot(a, b):
        return jnp.dot(a, b, preferred_element_type=jnp.float32)

    update = dot(high, lower_high[...]) + (dot(low, lower_high[...]) + dot(high, lower_low[...]))
    for row in range(COLS):
        out[row, 0:1, :] = child[row, 0:1, :] + update[row:row + 1, :]


def shards(ancestor_inverse, pattern, child_lower, child_diag_inv):
    params = pltpu.CompilerParams(vmem_limit_bytes=VMEM_LIMIT)
    own_rows = child_lower[0]
    pair = jnp.concatenate(
        [own_rows, lax.ppermute(own_rows, "pcol", [(0, 2), (1, 3), (2, 0), (3, 1)])], axis=0
    )
    spread = pl.pallas_call(
        spread_kernel,
        out_shape=jax.ShapeDtypeStruct((N_LEAF, PIECE1, BLK), jnp.float32),
        in_specs=in_vmem(2),
        out_specs=in_vmem(1)[0],
        compiler_params=params,
    )(ancestor_inverse, pattern)
    pair, spread = lax.optimization_barrier((pair, spread))
    lower_own = lax.all_gather(pair, "prow", axis=0, tiled=True)
    spread = lax.all_to_all(spread, "leaf", 0, 0, tiled=True)
    chosen = pl.pallas_call(
        select_kernel,
        out_shape=jax.ShapeDtypeStruct((N_LEAF, PIECE2, BLK), jnp.float32),
        in_specs=in_vmem(1),
        out_specs=in_vmem(1)[0],
        scratch_shapes=[pltpu.SMEM((N_LEAF, 1, BLK), jnp.float32), pltpu.SemaphoreType.DMA(())],
        compiler_params=params,
    )(spread)
    chosen = lax.all_to_all(chosen, "leaf", 0, 0, tiled=True)
    lower_own, chosen = lax.optimization_barrier((lower_own, chosen))
    lower_other = lax.ppermute(lower_own, "pcol", [(0, 1), (1, 0), (2, 3), (3, 2)])
    cross, pieces, lower_high, lower_low = pl.pallas_call(
        cross_kernel,
        out_shape=(
            jax.ShapeDtypeStruct((1, ROWS, S1), jnp.float32),
            jax.ShapeDtypeStruct((N_GRID, PIECE3, BLK), jnp.float32),
            jax.ShapeDtypeStruct((NP * BLK, S1), jnp.bfloat16),
            jax.ShapeDtypeStruct((NP * BLK, S1), jnp.bfloat16),
        ),
        in_specs=in_vmem(3),
        out_specs=tuple(in_vmem(4)),
        scratch_shapes=[
            pltpu.VMEM((ROWS, NP * BLK), jnp.float32),
            pltpu.VMEM((ROWS, S1), jnp.float32),
        ],
        compiler_params=params,
    )(chosen, lower_own.reshape(NP, 64, S1), lower_other.reshape(NP, 64, S1))
    pieces = lax.all_to_all(pieces, ("prow", "pcol"), 0, 0, tiled=True)
    diagonal = pl.pallas_call(
        diagonal_kernel,
        out_shape=jax.ShapeDtypeStruct((COLS, 1, S1), jnp.float32),
        in_specs=[pl.BlockSpec(memory_space=pltpu.SMEM)] + in_vmem(4),
        out_specs=in_vmem(1)[0],
        scratch_shapes=[pltpu.VMEM((32, NP * BLK), jnp.float32)],
        compiler_params=params,
    )(pattern, pieces, lower_high, lower_low, jnp.transpose(child_diag_inv, (1, 0, 2)))
    return cross, jnp.transpose(diagonal, (1, 0, 2))


def solution(mesh):
    return jax.shard_map(
        shards,
        mesh=mesh,
        in_specs=(
            P(("prow", "pcol"), "leaf"),
            P("leaf", None),
            P("leaf", ("prow", "pcol"), None),
            P("leaf", ("prow", "pcol"), None),
        ),
        out_specs=(P("leaf", ("prow", "pcol"), None), P("leaf", ("prow", "pcol"), None)),
        check_vma=False,
    )
```

```python
import jax
import jax.numpy as jnp
from jax import lax
from jax.experimental import pallas as pl
from jax.experimental.pallas import tpu as pltpu
from jax.sharding import Mesh
from jax.sharding import PartitionSpec as P

BLK = 128
NP = 8
N_LEAF = 16
N_GRID = 32
ROWS = 192
CHUNK = ROWS // N_LEAF
OWN_BLOCKS = 3
S1 = 896
COLS = S1 // N_GRID
LROWS = 32
PAT_ROW = OWN_BLOCKS * CHUNK
PIECE1 = 40
PIECE2 = NP * CHUNK
HALF = COLS // 2
PIECE3 = COLS + HALF
VMEM_LIMIT = 16 * 1024 * 1024
CROSS_LIMIT = 52 * 1024 * 1024


GRID = ("prow", "side", "core")


def in_vmem(count):
    return [pl.BlockSpec(memory_space=pltpu.VMEM)] * count


def split(value):
    high = value.astype(jnp.bfloat16)
    low = (value - high.astype(jnp.float32)).astype(jnp.bfloat16)
    return high, low


def spread_kernel(ancestor, pattern, out):
    row = pattern[...].astype(jnp.float32)
    for leaf in range(N_LEAF):
        for block in range(OWN_BLOCKS):
            out[leaf, block * CHUNK:(block + 1) * CHUNK, :] = ancestor[
                leaf * CHUNK:(leaf + 1) * CHUNK, block * BLK:(block + 1) * BLK
            ]
        out[leaf, PAT_ROW:PIECE1, :] = jnp.zeros((PIECE1 - PAT_ROW, BLK), jnp.float32)
        out[leaf, PAT_ROW:PAT_ROW + 1, 0:NP] = row


def select_kernel(pieces, out, patterns, semaphore):
    copy = pltpu.make_async_copy(pieces.at[:, PAT_ROW:PAT_ROW + 1, :], patterns, semaphore)
    copy.start()
    copy.wait()

    def one_leaf(leaf, carry):
        for block in range(NP):
            number = patterns[leaf, 0, block].astype(jnp.int32)
            owner = number // OWN_BLOCKS
            first = (number - owner * OWN_BLOCKS) * CHUNK
            out[leaf, block * CHUNK:(block + 1) * CHUNK, :] = pieces[owner, pl.ds(first, CHUNK), :]
        return carry

    lax.fori_loop(0, N_LEAF, one_leaf, 0)


def cross_kernel(pieces, lower, cross, out, lower_high, lower_low, panel, product, held, semaphores):
    core = lax.axis_index("core")
    side = lax.axis_index("side")
    copies = [
        pltpu.make_async_copy(lower.at[block], held.at[block], semaphores.at[block])
        for block in range(NP)
    ]
    for copy in copies:
        copy.start()
    for leaf in range(N_LEAF):
        for block in range(NP):
            panel[leaf * CHUNK:(leaf + 1) * CHUNK, block * BLK:(block + 1) * BLK] = pieces[
                leaf, block * CHUNK:(block + 1) * CHUNK, :
            ]
    panel_high, panel_low = split(panel[...])
    for block in range(NP):
        copies[block].wait()
        for at_core in range(2):
            for part, at_side in ((0, side), (1, 1 - side)):
                row = at_core * 64 + part * LROWS
                high, low = split(held[block, row:row + LROWS, :])
                first = pl.multiple_of(block * BLK + at_side * 64 + at_core * LROWS, LROWS)
                lower_high[pl.ds(first, LROWS), :] = high
                lower_low[pl.ds(first, LROWS), :] = low

    def dot(a, b):
        return jnp.dot(a, b, preferred_element_type=jnp.float32)

    value = dot(panel_high, lower_high[...]) + (
        dot(panel_low, lower_high[...]) + dot(panel_high, lower_low[...])
    )
    product[...] = value
    cross[0, :, :] = -value
    whole = product[pl.ds(pl.multiple_of(core * 64, 64), BLK), :].T
    half = product[pl.ds(pl.multiple_of((1 - core) * BLK, BLK), 64), :].T
    for device in range(N_GRID):
        at = device * COLS
        first = device * PIECE3
        out[first:first + COLS, :] = whole[at:at + COLS, :]
        out[first + COLS:first + PIECE3, 0:64] = half[at:at + HALF, :]
        out[first + COLS:first + PIECE3, 64:128] = half[at + HALF:at + COLS, :]


def diagonal_kernel(pattern, pieces, lower_high, lower_low, child, out, rows):
    lane = lax.broadcasted_iota(jnp.int32, (HALF, BLK), 1)
    for block in range(NP):
        number = pattern[0, block]
        group = number // 3
        place = number - group * 3
        upper = 2 * group
        middle = place == 1
        whole = pieces[pl.ds((upper + place // 2) * PIECE3, COLS), :]
        first = pieces[pl.ds(upper * PIECE3 + COLS, HALF), :]
        second = pieces[pl.ds((upper + 1) * PIECE3 + COLS, HALF), :]
        top = jnp.where(lane < 64, first, pltpu.roll(second, 64, 1))
        bottom = jnp.where(lane < 64, pltpu.roll(first, 64, 1), second)
        here = slice(block * BLK, (block + 1) * BLK)
        rows[0:HALF, here] = jnp.where(middle, top, whole[0:HALF, :])
        rows[HALF:COLS, here] = jnp.where(middle, bottom, whole[HALF:COLS, :])
    rows[COLS:, :] = jnp.zeros((32 - COLS, NP * BLK), jnp.float32)
    high, low = split(rows[...])

    def dot(a, b):
        return jnp.dot(a, b, preferred_element_type=jnp.float32)

    update = dot(high, lower_high[...]) + (dot(low, lower_high[...]) + dot(high, lower_low[...]))
    for row in range(COLS):
        out[row, 0:1, :] = child[row, 0:1, :] + update[row:row + 1, :]


def shards(ancestor_inverse, pattern, child_lower, child_diag_inv):
    params = pltpu.CompilerParams(vmem_limit_bytes=VMEM_LIMIT)
    own_rows = child_lower[0]
    pair = jnp.concatenate(
        [own_rows, lax.ppermute(own_rows, "side", [(0, 1), (1, 0)])], axis=0
    )
    spread = pl.pallas_call(
        spread_kernel,
        out_shape=jax.ShapeDtypeStruct((N_LEAF, PIECE1, BLK), jnp.float32),
        in_specs=in_vmem(2),
        out_specs=in_vmem(1)[0],
        compiler_params=params,
    )(ancestor_inverse, pattern)
    pair, spread = lax.optimization_barrier((pair, spread))
    lower = lax.all_gather(pair, ("prow", "core"), axis=0, tiled=True)
    spread = lax.all_to_all(spread, "leaf", 0, 0, tiled=True)
    chosen = pl.pallas_call(
        select_kernel,
        out_shape=jax.ShapeDtypeStruct((N_LEAF, PIECE2, BLK), jnp.float32),
        in_specs=in_vmem(1),
        out_specs=in_vmem(1)[0],
        scratch_shapes=[pltpu.SMEM((N_LEAF, 1, BLK), jnp.float32), pltpu.SemaphoreType.DMA(())],
        compiler_params=params,
    )(spread)
    chosen = lax.all_to_all(chosen, "leaf", 0, 0, tiled=True)
    cross, pieces, lower_high, lower_low = pl.pallas_call(
        cross_kernel,
        out_shape=(
            jax.ShapeDtypeStruct((1, ROWS, S1), jnp.float32),
            jax.ShapeDtypeStruct((N_GRID * PIECE3, BLK), jnp.float32),
            jax.ShapeDtypeStruct((NP * BLK, S1), jnp.bfloat16),
            jax.ShapeDtypeStruct((NP * BLK, S1), jnp.bfloat16),
        ),
        in_specs=in_vmem(1) + [pl.BlockSpec(memory_space=pltpu.HBM)],
        out_specs=tuple(in_vmem(4)),
        scratch_shapes=[
            pltpu.VMEM((ROWS, NP * BLK), jnp.float32),
            pltpu.VMEM((ROWS, S1), jnp.float32),
            pltpu.VMEM((NP, BLK, S1), jnp.float32),
            pltpu.SemaphoreType.DMA((NP,)),
        ],
        compiler_params=pltpu.CompilerParams(vmem_limit_bytes=CROSS_LIMIT),
    )(chosen, lower.reshape(NP, BLK, S1))
    pieces = lax.all_to_all(
        pieces.reshape(N_GRID, PIECE3, 1, BLK), GRID, 0, 0, tiled=True
    ).reshape(N_GRID * PIECE3, BLK)
    diagonal = pl.pallas_call(
        diagonal_kernel,
        out_shape=jax.ShapeDtypeStruct((COLS, 1, S1), jnp.float32),
        in_specs=[pl.BlockSpec(memory_space=pltpu.SMEM)] + in_vmem(4),
        out_specs=in_vmem(1)[0],
        scratch_shapes=[pltpu.VMEM((32, NP * BLK), jnp.float32)],
        compiler_params=params,
    )(pattern, pieces, lower_high, lower_low, jnp.transpose(child_diag_inv, (1, 0, 2)))
    return cross, jnp.transpose(diagonal, (1, 0, 2))


def solution(mesh):
    shape = mesh.shape
    parts = Mesh(
        mesh.devices.reshape(shape["leaf"], shape["prow"], shape["pcol"] // 2, 2), ("leaf",) + GRID
    )
    return jax.shard_map(
        shards,
        mesh=parts,
        in_specs=(
            P(GRID, "leaf"),
            P("leaf", None),
            P("leaf", GRID, None),
            P("leaf", GRID, None),
        ),
        out_specs=(P("leaf", GRID, None), P("leaf", GRID, None)),
        check_vma=False,
    )
```

```python
import jax
import jax.numpy as jnp
from jax import lax
from jax.experimental import pallas as pl
from jax.experimental.pallas import tpu as pltpu
from jax.sharding import Mesh
from jax.sharding import PartitionSpec as P

BLK = 128
NP = 8
N_LEAF = 16
N_GRID = 32
ROWS = 192
CHUNK = ROWS // N_LEAF
OWN_BLOCKS = 3
S1 = 896
COLS = S1 // N_GRID
LROWS = 32
PAT_ROW = OWN_BLOCKS * CHUNK
PIECE1 = 40
PIECE2 = NP * CHUNK
HALF = COLS // 2
PIECE3 = COLS + HALF
VMEM_LIMIT = 16 * 1024 * 1024
CROSS_LIMIT = 48 * 1024 * 1024


GRID = ("prow", "side", "core")


def in_vmem(count):
    return [pl.BlockSpec(memory_space=pltpu.VMEM)] * count


def split(value):
    high = value.astype(jnp.bfloat16)
    low = (value - high.astype(jnp.float32)).astype(jnp.bfloat16)
    return high, low


def spread_kernel(ancestor, pattern, lower, out, kept):
    kept[...] = lower[...]
    row = pattern[...].astype(jnp.float32)
    for leaf in range(N_LEAF):
        for block in range(OWN_BLOCKS):
            out[leaf, block * CHUNK:(block + 1) * CHUNK, :] = ancestor[
                leaf * CHUNK:(leaf + 1) * CHUNK, block * BLK:(block + 1) * BLK
            ]
        out[leaf, PAT_ROW:PIECE1, :] = jnp.zeros((PIECE1 - PAT_ROW, BLK), jnp.float32)
        out[leaf, PAT_ROW:PAT_ROW + 1, 0:NP] = row


def pair_kernel(own, received, out, semaphores):
    first = pltpu.make_async_copy(own, out.at[0:LROWS, :], semaphores.at[0])
    second = pltpu.make_async_copy(received, out.at[LROWS:2 * LROWS, :], semaphores.at[1])
    first.start()
    second.start()
    first.wait()
    second.wait()


def select_kernel(pieces, out, patterns, semaphore):
    copy = pltpu.make_async_copy(pieces.at[:, PAT_ROW:PAT_ROW + 1, :], patterns, semaphore)
    copy.start()
    copy.wait()

    for leaf in range(N_LEAF):
        for block in range(NP):
            number = patterns[leaf, 0, block].astype(jnp.int32)
            owner = number // OWN_BLOCKS
            first = (number - owner * OWN_BLOCKS) * CHUNK
            out[leaf, block * CHUNK:(block + 1) * CHUNK, :] = pieces[owner, pl.ds(first, CHUNK), :]


def panel_kernel(pieces, high, low, panel):
    for leaf in range(N_LEAF):
        for block in range(NP):
            panel[leaf * CHUNK:(leaf + 1) * CHUNK, block * BLK:(block + 1) * BLK] = pieces[
                leaf, block * CHUNK:(block + 1) * CHUNK, :
            ]
    high[...], low[...] = split(panel[...])


def cross_kernel(panel_high, panel_low, lower, cross, out, lower_high, lower_low, product, held, semaphores):
    core = lax.axis_index("core")
    side = lax.axis_index("side")
    copies = [
        pltpu.make_async_copy(lower.at[block], held.at[block], semaphores.at[block])
        for block in range(NP)
    ]
    for copy in copies:
        copy.start()
    for block in range(NP):
        copies[block].wait()
        for at_core in range(2):
            for part, at_side in ((0, side), (1, 1 - side)):
                row = at_core * 64 + part * LROWS
                high, low = split(held[block, row:row + LROWS, :])
                first = pl.multiple_of(block * BLK + at_side * 64 + at_core * LROWS, LROWS)
                lower_high[pl.ds(first, LROWS), :] = high
                lower_low[pl.ds(first, LROWS), :] = low

    def dot(a, b):
        return jnp.dot(a, b, preferred_element_type=jnp.float32)

    value = dot(panel_high[...], lower_high[...]) + (
        dot(panel_low[...], lower_high[...]) + dot(panel_high[...], lower_low[...])
    )
    product[...] = value
    cross[0, :, :] = -value
    whole = product[pl.ds(pl.multiple_of(core * 64, 64), BLK), :].T
    half = product[pl.ds(pl.multiple_of((1 - core) * BLK, BLK), 64), :].T
    for device in range(N_GRID):
        at = device * COLS
        first = device * PIECE3
        out[first:first + COLS, :] = whole[at:at + COLS, :]
        out[first + COLS:first + PIECE3, 0:64] = half[at:at + HALF, :]
        out[first + COLS:first + PIECE3, 64:128] = half[at + HALF:at + COLS, :]


def diagonal_kernel(pattern, pieces, lower_high, lower_low, child, out, rows):
    lane = lax.broadcasted_iota(jnp.int32, (HALF, BLK), 1)
    for block in range(NP):
        number = pattern[0, block]
        group = number // 3
        place = number - group * 3
        upper = 2 * group
        middle = place == 1
        whole = pieces[pl.ds((upper + place // 2) * PIECE3, COLS), :]
        first = pieces[pl.ds(upper * PIECE3 + COLS, HALF), :]
        second = pieces[pl.ds((upper + 1) * PIECE3 + COLS, HALF), :]
        top = jnp.where(lane < 64, first, pltpu.roll(second, 64, 1))
        bottom = jnp.where(lane < 64, pltpu.roll(first, 64, 1), second)
        here = slice(block * BLK, (block + 1) * BLK)
        rows[0:HALF, here] = jnp.where(middle, top, whole[0:HALF, :])
        rows[HALF:COLS, here] = jnp.where(middle, bottom, whole[HALF:COLS, :])
    rows[COLS:, :] = jnp.zeros((32 - COLS, NP * BLK), jnp.float32)
    high, low = split(rows[...])

    def dot(a, b):
        return jnp.dot(a, b, preferred_element_type=jnp.float32)

    update = dot(high, lower_high[...]) + (dot(low, lower_high[...]) + dot(high, lower_low[...]))
    for row in range(COLS):
        out[row, 0:1, :] = child[row, 0:1, :] + update[row:row + 1, :]


def shards(ancestor_inverse, pattern, child_lower, child_diag_inv):
    params = pltpu.CompilerParams(vmem_limit_bytes=VMEM_LIMIT)
    own_rows = child_lower[0]
    received = lax.ppermute(own_rows, "side", [(0, 1), (1, 0)])
    spread, kept = pl.pallas_call(
        spread_kernel,
        out_shape=(
            jax.ShapeDtypeStruct((N_LEAF, PIECE1, BLK), jnp.float32),
            jax.ShapeDtypeStruct((LROWS, S1), jnp.float32),
        ),
        in_specs=in_vmem(3),
        out_specs=tuple(in_vmem(2)),
        compiler_params=params,
    )(ancestor_inverse, pattern, own_rows)
    spread, received = lax.optimization_barrier((spread, received))
    pair = pl.pallas_call(
        pair_kernel,
        out_shape=jax.ShapeDtypeStruct((2 * LROWS, S1), jnp.float32),
        in_specs=[pl.BlockSpec(memory_space=pl.ANY)] * 2,
        out_specs=pl.BlockSpec(memory_space=pltpu.HBM),
        scratch_shapes=[pltpu.SemaphoreType.DMA((2,))],
        compiler_params=params,
    )(kept, received)
    pair, spread = lax.optimization_barrier((pair, spread))
    lower = lax.all_gather(pair, ("prow", "core"), axis=0, tiled=True)
    spread = lax.all_to_all(spread, "leaf", 0, 0, tiled=True)
    chosen = pl.pallas_call(
        select_kernel,
        out_shape=jax.ShapeDtypeStruct((N_LEAF, PIECE2, BLK), jnp.float32),
        in_specs=in_vmem(1),
        out_specs=in_vmem(1)[0],
        scratch_shapes=[pltpu.SMEM((N_LEAF, 1, BLK), jnp.float32), pltpu.SemaphoreType.DMA(())],
        compiler_params=params,
    )(spread)
    chosen = lax.all_to_all(chosen, "leaf", 0, 0, tiled=True)
    panel_high, panel_low = pl.pallas_call(
        panel_kernel,
        out_shape=(jax.ShapeDtypeStruct((ROWS, NP * BLK), jnp.bfloat16),) * 2,
        in_specs=in_vmem(1),
        out_specs=tuple(in_vmem(2)),
        scratch_shapes=[pltpu.VMEM((ROWS, NP * BLK), jnp.float32)],
        compiler_params=params,
    )(chosen)
    cross, pieces, lower_high, lower_low = pl.pallas_call(
        cross_kernel,
        out_shape=(
            jax.ShapeDtypeStruct((1, ROWS, S1), jnp.float32),
            jax.ShapeDtypeStruct((N_GRID * PIECE3, BLK), jnp.float32),
            jax.ShapeDtypeStruct((NP * BLK, S1), jnp.bfloat16),
            jax.ShapeDtypeStruct((NP * BLK, S1), jnp.bfloat16),
        ),
        in_specs=in_vmem(2) + [pl.BlockSpec(memory_space=pltpu.HBM)],
        out_specs=tuple(in_vmem(4)),
        scratch_shapes=[
            pltpu.VMEM((ROWS, S1), jnp.float32),
            pltpu.VMEM((NP, BLK, S1), jnp.float32),
            pltpu.SemaphoreType.DMA((NP,)),
        ],
        compiler_params=pltpu.CompilerParams(vmem_limit_bytes=CROSS_LIMIT),
    )(panel_high, panel_low, lower.reshape(NP, BLK, S1))
    pieces = lax.all_to_all(
        pieces.reshape(N_GRID, PIECE3, 1, BLK), GRID, 0, 0, tiled=True
    ).reshape(N_GRID * PIECE3, BLK)
    diagonal = pl.pallas_call(
        diagonal_kernel,
        out_shape=jax.ShapeDtypeStruct((COLS, 1, S1), jnp.float32),
        in_specs=[pl.BlockSpec(memory_space=pltpu.SMEM)] + in_vmem(4),
        out_specs=in_vmem(1)[0],
        scratch_shapes=[pltpu.VMEM((32, NP * BLK), jnp.float32)],
        compiler_params=params,
    )(pattern, pieces, lower_high, lower_low, jnp.transpose(child_diag_inv, (1, 0, 2)))
    return cross, jnp.transpose(diagonal, (1, 0, 2))


def solution(mesh):
    shape = mesh.shape
    parts = Mesh(
        mesh.devices.reshape(shape["leaf"], shape["prow"], shape["pcol"] // 2, 2), ("leaf",) + GRID
    )
    return jax.shard_map(
        shards,
        mesh=parts,
        in_specs=(
            P(GRID, "leaf"),
            P("leaf", None),
            P("leaf", GRID, None),
            P("leaf", GRID, None),
        ),
        out_specs=(P("leaf", GRID, None), P("leaf", GRID, None)),
        check_vma=False,
    )
```

```python
import jax
import jax.numpy as jnp
from jax import lax
from jax.experimental import pallas as pl
from jax.experimental.pallas import tpu as pltpu
from jax.sharding import Mesh
from jax.sharding import PartitionSpec as P

BLK = 128
NP = 8
N_LEAF = 16
N_GRID = 32
ROWS = 192
CHUNK = ROWS // N_LEAF
OWN_BLOCKS = 3
S1 = 896
COLS = S1 // N_GRID
LROWS = 32
SELECT_PARTS = 4
PAT_ROW = OWN_BLOCKS * CHUNK
PIECE1 = 40
PIECE2 = NP * CHUNK
HALF = COLS // 2
PIECE3 = COLS + HALF
VMEM_LIMIT = 16 * 1024 * 1024
CROSS_LIMIT = 16 * 1024 * 1024


GRID = ("prow", "side", "core")


STEPS = ((0, 2), (1, 3), (-1, -3), (-2, 4))


def from_row(value, distance):
    return lax.ppermute(value, "prow", [(at, (at - distance) % NP) for at in range(NP)])


def swap_side(value):
    return lax.ppermute(value, "side", [(0, 1), (1, 0)])


def hint(microseconds):
    return pl.CostEstimate(flops=int(microseconds * 1.1e9), bytes_accessed=int(microseconds * 3.7e6), transcendentals=0)


def in_vmem(count):
    return [pl.BlockSpec(memory_space=pltpu.VMEM)] * count


def split(value):
    high = value.astype(jnp.bfloat16)
    low = (value - high.astype(jnp.float32)).astype(jnp.bfloat16)
    return high, low


def spread_kernel(ancestor, pattern, out):
    row = pattern[...].astype(jnp.float32)
    for leaf in range(N_LEAF):
        for block in range(OWN_BLOCKS):
            out[leaf, block * CHUNK:(block + 1) * CHUNK, :] = ancestor[
                leaf * CHUNK:(leaf + 1) * CHUNK, block * BLK:(block + 1) * BLK
            ]
        out[leaf, PAT_ROW:PIECE1, :] = jnp.zeros((PIECE1 - PAT_ROW, BLK), jnp.float32)
        out[leaf, PAT_ROW:PAT_ROW + 1, 0:NP] = row


def pair_kernel(own, across, out):
    out[0:LROWS, :] = own[...]
    out[LROWS:2 * LROWS, :] = across[...]


def stack(out, *parts):
    first = 0
    for part in parts:
        rows = part.shape[0]
        out[first:first + rows, :] = part[...]
        first += rows


def near_kernel(pair, ahead, behind, up, down, up_half, down_half):
    stack(up, pair, ahead)
    stack(down, pair, behind)
    up_half[...] = ahead[0:LROWS, :]
    down_half[...] = behind[LROWS:2 * LROWS, :]


def far_kernel(*refs):
    stack(refs[-1], *refs[:-1])


def select_kernel(pieces, out, held, chosen, patterns, semaphores):
    copies = [
        pltpu.make_async_copy(pieces, held, semaphores.at[0]),
        pltpu.make_async_copy(pieces.at[:, PAT_ROW:PAT_ROW + 1, :], patterns, semaphores.at[1]),
    ]
    for copy in copies:
        copy.start()
    for copy in copies:
        copy.wait()
    sent = []
    for part in range(SELECT_PARTS):
        count = N_LEAF // SELECT_PARTS
        for leaf in range(part * count, (part + 1) * count):
            for block in range(NP):
                number = patterns[leaf, 0, block].astype(jnp.int32)
                owner = number // OWN_BLOCKS
                first = (number - owner * OWN_BLOCKS) * CHUNK
                chosen[leaf, block * CHUNK:(block + 1) * CHUNK, :] = held[
                    owner, pl.ds(first, CHUNK), :
                ]
        here = pl.ds(part * count, count)
        sent.append(pltpu.make_async_copy(chosen.at[here], out.at[here], semaphores.at[2 + part]))
        sent[-1].start()
    for copy in sent:
        copy.wait()


def panel_kernel(pieces, high, low, panel):
    for leaf in range(N_LEAF):
        for block in range(NP):
            panel[leaf * CHUNK:(leaf + 1) * CHUNK, block * BLK:(block + 1) * BLK] = pieces[
                leaf, block * CHUNK:(block + 1) * CHUNK, :
            ]
    high[...], low[...] = split(panel[...])


def cross_kernel(panel_high, panel_low, *refs):
    sources = refs[:2 * len(STEPS)]
    cross, out, lower_high, lower_low, product = refs[2 * len(STEPS):]
    core = lax.axis_index("core")
    side = lax.axis_index("side")
    place = lax.axis_index("prow")
    for at, source in enumerate(sources):
        at_core = core if at < len(STEPS) else 1 - core
        for group, step in enumerate(STEPS[at % len(STEPS)]):
            block = lax.rem(place + step + NP, NP)
            for part, at_side in ((0, side), (1, 1 - side)):
                row = group * 64 + part * LROWS
                high, low = split(source[row:row + LROWS, :])
                first = pl.multiple_of(block * BLK + at_side * 64 + at_core * LROWS, LROWS)
                lower_high[pl.ds(first, LROWS), :] = high
                lower_low[pl.ds(first, LROWS), :] = low

    def dot(a, b):
        return jnp.dot(a, b, preferred_element_type=jnp.float32)

    value = dot(panel_high[...], lower_high[...]) + (
        dot(panel_low[...], lower_high[...]) + dot(panel_high[...], lower_low[...])
    )
    product[...] = value
    cross[0, :, :] = -value
    whole = product[pl.ds(pl.multiple_of(core * 64, 64), BLK), :].T
    half = product[pl.ds(pl.multiple_of((1 - core) * BLK, BLK), 64), :].T
    for device in range(N_GRID):
        at = device * COLS
        first = device * PIECE3
        out[first:first + COLS, :] = whole[at:at + COLS, :]
        out[first + COLS:first + PIECE3, 0:64] = half[at:at + HALF, :]
        out[first + COLS:first + PIECE3, 64:128] = half[at + HALF:at + COLS, :]


def diagonal_kernel(pattern, pieces, lower_high, lower_low, child, out, rows):
    lane = lax.broadcasted_iota(jnp.int32, (HALF, BLK), 1)
    for block in range(NP):
        number = pattern[0, block]
        group = number // 3
        place = number - group * 3
        upper = 2 * group
        middle = place == 1
        whole = pieces[pl.ds((upper + place // 2) * PIECE3, COLS), :]
        first = pieces[pl.ds(upper * PIECE3 + COLS, HALF), :]
        second = pieces[pl.ds((upper + 1) * PIECE3 + COLS, HALF), :]
        top = jnp.where(lane < 64, first, pltpu.roll(second, 64, 1))
        bottom = jnp.where(lane < 64, pltpu.roll(first, 64, 1), second)
        here = slice(block * BLK, (block + 1) * BLK)
        rows[0:HALF, here] = jnp.where(middle, top, whole[0:HALF, :])
        rows[HALF:COLS, here] = jnp.where(middle, bottom, whole[HALF:COLS, :])
    rows[COLS:, :] = jnp.zeros((32 - COLS, NP * BLK), jnp.float32)
    high, low = split(rows[...])

    def dot(a, b):
        return jnp.dot(a, b, preferred_element_type=jnp.float32)

    update = dot(high, lower_high[...]) + (dot(low, lower_high[...]) + dot(high, lower_low[...]))
    for row in range(COLS):
        out[row, 0:1, :] = child[row, 0:1, :] + update[row:row + 1, :]


def call(kernel, rows, microseconds, *parts):
    return pl.pallas_call(
        kernel,
        out_shape=tuple(jax.ShapeDtypeStruct((count, S1), jnp.float32) for count in rows),
        in_specs=in_vmem(len(parts)),
        out_specs=tuple(in_vmem(len(rows))),
        cost_estimate=hint(microseconds),
        compiler_params=pltpu.CompilerParams(vmem_limit_bytes=VMEM_LIMIT),
    )(*parts)


def shards(ancestor_inverse, pattern, child_lower, child_diag_inv):
    params = pltpu.CompilerParams(vmem_limit_bytes=VMEM_LIMIT)
    own = child_lower[0]
    spread = pl.pallas_call(
        spread_kernel,
        out_shape=jax.ShapeDtypeStruct((N_LEAF, PIECE1, BLK), jnp.float32),
        in_specs=in_vmem(2),
        out_specs=in_vmem(1)[0],
        compiler_params=params,
    )(ancestor_inverse, pattern)
    across = swap_side(own)
    pair = pl.pallas_call(
        pair_kernel,
        out_shape=jax.ShapeDtypeStruct((64, S1), jnp.float32),
        in_specs=in_vmem(2),
        out_specs=in_vmem(1)[0],
        cost_estimate=hint(2000),
        compiler_params=params,
    )(own, across)
    ahead, behind = from_row(pair, 2), from_row(pair, -2)
    spread = lax.all_to_all(spread, "leaf", 0, 0, tiled=True)
    chosen = pl.pallas_call(
        select_kernel,
        out_shape=jax.ShapeDtypeStruct((N_LEAF, PIECE2, BLK), jnp.float32),
        in_specs=[pl.BlockSpec(memory_space=pl.ANY)],
        out_specs=pl.BlockSpec(memory_space=pl.ANY),
        scratch_shapes=[
            pltpu.VMEM((N_LEAF, PIECE1, BLK), jnp.float32),
            pltpu.VMEM((N_LEAF, PIECE2, BLK), jnp.float32),
            pltpu.SMEM((N_LEAF, 1, BLK), jnp.float32),
            pltpu.SemaphoreType.DMA((2 + SELECT_PARTS,)),
        ],
        compiler_params=params,
    )(spread)
    chosen = lax.all_to_all(chosen, "leaf", 0, 0, tiled=True)
    up, down, up_half, down_half = call(near_kernel, (128, 128, 32, 32), 2000, pair, ahead, behind)
    (far,) = call(far_kernel, (128,), 0, behind, from_row(up_half, 2), from_row(down_half, -2))
    mine = [up, from_row(up, 1), from_row(down, -1), far]
    other = [lax.ppermute(value, "core", [(0, 1), (1, 0)]) for value in mine]
    panel_high, panel_low = pl.pallas_call(
        panel_kernel,
        out_shape=(jax.ShapeDtypeStruct((ROWS, NP * BLK), jnp.bfloat16),) * 2,
        in_specs=in_vmem(1),
        out_specs=tuple(in_vmem(2)),
        scratch_shapes=[pltpu.VMEM((ROWS, NP * BLK), jnp.float32)],
        compiler_params=params,
    )(chosen)
    cross, pieces, lower_high, lower_low = pl.pallas_call(
        cross_kernel,
        out_shape=(
            jax.ShapeDtypeStruct((1, ROWS, S1), jnp.float32),
            jax.ShapeDtypeStruct((N_GRID * PIECE3, BLK), jnp.float32),
            jax.ShapeDtypeStruct((NP * BLK, S1), jnp.bfloat16),
            jax.ShapeDtypeStruct((NP * BLK, S1), jnp.bfloat16),
        ),
        in_specs=in_vmem(10),
        out_specs=tuple(in_vmem(4)),
        scratch_shapes=[
            pltpu.VMEM((ROWS, S1), jnp.float32),
        ],
        compiler_params=pltpu.CompilerParams(vmem_limit_bytes=CROSS_LIMIT),
    )(panel_high, panel_low, *mine, *other)
    pieces = lax.all_to_all(
        pieces.reshape(N_GRID, PIECE3, 1, BLK), GRID, 0, 0, tiled=True
    ).reshape(N_GRID * PIECE3, BLK)
    diagonal = pl.pallas_call(
        diagonal_kernel,
        out_shape=jax.ShapeDtypeStruct((COLS, 1, S1), jnp.float32),
        in_specs=[pl.BlockSpec(memory_space=pltpu.SMEM)] + in_vmem(4),
        out_specs=in_vmem(1)[0],
        scratch_shapes=[pltpu.VMEM((32, NP * BLK), jnp.float32)],
        compiler_params=params,
    )(pattern, pieces, lower_high, lower_low, jnp.transpose(child_diag_inv, (1, 0, 2)))
    return cross, jnp.transpose(diagonal, (1, 0, 2))


def solution(mesh):
    shape = mesh.shape
    parts = Mesh(
        mesh.devices.reshape(shape["leaf"], shape["prow"], shape["pcol"] // 2, 2), ("leaf",) + GRID
    )
    return jax.shard_map(
        shards,
        mesh=parts,
        in_specs=(
            P(GRID, "leaf"),
            P("leaf", None),
            P("leaf", GRID, None),
            P("leaf", GRID, None),
        ),
        out_specs=(P("leaf", GRID, None), P("leaf", GRID, None)),
        check_vma=False,
    )
```

```python
import jax
import jax.numpy as jnp
from jax import lax
from jax.experimental import pallas as pl
from jax.experimental.pallas import tpu as pltpu
from jax.sharding import Mesh
from jax.sharding import PartitionSpec as P

BLK = 128
NP = 8
N_LEAF = 16
N_GRID = 32
ROWS = 192
CHUNK = ROWS // N_LEAF
OWN_BLOCKS = 3
S1 = 896
COLS = S1 // N_GRID
LROWS = 32
SELECT_PARTS = 4
PAT_ROW = OWN_BLOCKS * CHUNK
PIECE1 = 40
PIECE2 = NP * CHUNK
HALF = COLS // 2
PIECE3 = COLS + HALF
VMEM_LIMIT = 16 * 1024 * 1024
SPREAD_LIMIT = 63 * 1024 * 1024


GRID = ("prow", "side", "core")


STEPS = (0, 2, -2, 1, 3, -1, -3, 4)


def from_row(value, distance):
    return lax.ppermute(value, "prow", [(at, (at - distance) % NP) for at in range(NP)])


def swap_side(value):
    return lax.ppermute(value, "side", [(0, 1), (1, 0)])


def hint(microseconds):
    return pl.CostEstimate(flops=int(microseconds * 1.1e9), bytes_accessed=int(microseconds * 3.7e6), transcendentals=0)


def in_vmem(count):
    return [pl.BlockSpec(memory_space=pltpu.VMEM)] * count


def split(value):
    high = value.astype(jnp.bfloat16)
    low = (value - high.astype(jnp.float32)).astype(jnp.bfloat16)
    return high, low


def spread_kernel(ancestor, pattern, out, panel, numbers, semaphores):
    copies = [
        pltpu.make_async_copy(ancestor, panel, semaphores.at[0]),
        pltpu.make_async_copy(pattern, numbers, semaphores.at[1]),
    ]
    for copy in copies:
        copy.start()
    for copy in copies:
        copy.wait()
    row = numbers[...].astype(jnp.float32)
    for leaf in range(N_LEAF):
        for block in range(OWN_BLOCKS):
            out[leaf, block * CHUNK:(block + 1) * CHUNK, :] = panel[
                leaf * CHUNK:(leaf + 1) * CHUNK, block * BLK:(block + 1) * BLK
            ]
        out[leaf, PAT_ROW:PIECE1, :] = jnp.zeros((PIECE1 - PAT_ROW, BLK), jnp.float32)
        out[leaf, PAT_ROW:PAT_ROW + 1, 0:NP] = row


def pair_kernel(own, across, out):
    out[0:LROWS, :] = own[...]
    out[LROWS:2 * LROWS, :] = across[...]


def stack(out, *parts):
    first = 0
    for part in parts:
        rows = part.shape[0]
        out[first:first + rows, :] = part[...]
        first += rows


def near_kernel(pair, ahead, behind, near, rear):
    stack(near, pair, ahead, behind)
    rear[...] = behind[...]


def join_kernel(*refs):
    stack(refs[-1], *refs[:-1])


def select_kernel(pieces, out, held, chosen, patterns, semaphores):
    copies = [
        pltpu.make_async_copy(pieces, held, semaphores.at[0]),
        pltpu.make_async_copy(pieces.at[:, PAT_ROW:PAT_ROW + 1, :], patterns, semaphores.at[1]),
    ]
    for copy in copies:
        copy.start()
    for copy in copies:
        copy.wait()
    sent = []
    for part in range(SELECT_PARTS):
        count = N_LEAF // SELECT_PARTS
        for leaf in range(part * count, (part + 1) * count):
            for block in range(NP):
                number = patterns[leaf, 0, block].astype(jnp.int32)
                owner = number // OWN_BLOCKS
                first = (number - owner * OWN_BLOCKS) * CHUNK
                chosen[leaf, block * CHUNK:(block + 1) * CHUNK, :] = held[
                    owner, pl.ds(first, CHUNK), :
                ]
        here = pl.ds(part * count, count)
        sent.append(pltpu.make_async_copy(chosen.at[here], out.at[here], semaphores.at[2 + part]))
        sent[-1].start()
    for copy in sent:
        copy.wait()


def by_core(first, second):
    lane = lax.broadcasted_iota(jnp.int32, first.shape, 1)

    def even(value):
        return jnp.where(lane < 32, value, pltpu.roll(value, 96, 1))

    def odd(value):
        return jnp.where(lane < 32, pltpu.roll(value, 96, 1), pltpu.roll(value, 64, 1))

    cores = [
        jnp.where(lane < 64, pick(first), pltpu.roll(pick(second), 64, 1)) for pick in (even, odd)
    ]
    swap = lax.axis_index("core") == 1
    return jnp.where(swap, cores[1], cores[0]), jnp.where(swap, cores[0], cores[1])


def order_rows(source, high_out, low_out):
    side = lax.axis_index("side")
    place = lax.axis_index("prow")
    for group, step in enumerate(STEPS):
        block = lax.rem(place + step + NP, NP)
        for part, at_side in ((0, side), (1, 1 - side)):
            row = group * 64 + part * LROWS
            high, low = split(source[row:row + LROWS, :])
            first = pl.multiple_of(block * 64 + at_side * LROWS, LROWS)
            high_out[pl.ds(first, LROWS), :] = high
            low_out[pl.ds(first, LROWS), :] = low


def multiply(high, low, lower_high, lower_low):
    def dot(a, b):
        return jnp.dot(a[...], b[...], preferred_element_type=jnp.float32)

    return dot(high, lower_high) + (dot(low, lower_high) + dot(high, lower_low))


def own_kernel(
    pieces, lower, partial, other_high, other_low, lower_high, lower_low, panel, own_high, own_low
):
    for leaf in range(N_LEAF):
        for block in range(NP):
            panel[leaf * CHUNK:(leaf + 1) * CHUNK, block * BLK:(block + 1) * BLK] = pieces[
                leaf, block * CHUNK:(block + 1) * CHUNK, :
            ]
    for at in range(NP // 2):
        here = slice(at * BLK, (at + 1) * BLK)
        own, other = by_core(
            panel[:, 2 * at * BLK:(2 * at + 1) * BLK], panel[:, (2 * at + 1) * BLK:(2 * at + 2) * BLK]
        )
        own_high[:, here], own_low[:, here] = split(own)
        other_high[:, here], other_low[:, here] = split(other)
    order_rows(lower, lower_high, lower_low)
    partial[...] = multiply(own_high, own_low, lower_high, lower_low)


def cross_kernel(partial, high, low, lower, cross, out, lower_high, lower_low, product):
    core = lax.axis_index("core")
    order_rows(lower, lower_high, lower_low)
    value = partial[...] + multiply(high, low, lower_high, lower_low)
    product[...] = value
    cross[0, :, :] = -value
    whole = product[pl.ds(pl.multiple_of(core * 64, 64), BLK), :].T
    half = product[pl.ds(pl.multiple_of((1 - core) * BLK, BLK), 64), :].T
    for device in range(N_GRID):
        at = device * COLS
        first = device * PIECE3
        out[first:first + COLS, :] = whole[at:at + COLS, :]
        out[first + COLS:first + PIECE3, 0:64] = half[at:at + HALF, :]
        out[first + COLS:first + PIECE3, 64:128] = half[at + HALF:at + COLS, :]


def diagonal_kernel(
    pattern, pieces, own_high, own_low, other_high, other_low, child, out, rows, *parts
):
    lane = lax.broadcasted_iota(jnp.int32, (HALF, BLK), 1)
    rows[:, COLS:, :] = jnp.zeros((NP, 32 - COLS, BLK), jnp.float32)
    for block in range(NP):
        number = pattern[0, block]
        group = number // 3
        place = number - group * 3
        upper = 2 * group
        middle = place == 1
        whole = pieces[pl.ds((upper + place // 2) * PIECE3, COLS), :]
        first = pieces[pl.ds(upper * PIECE3 + COLS, HALF), :]
        second = pieces[pl.ds((upper + 1) * PIECE3 + COLS, HALF), :]
        top = jnp.where(lane < 64, first, pltpu.roll(second, 64, 1))
        bottom = jnp.where(lane < 64, pltpu.roll(first, 64, 1), second)
        rows[block, 0:HALF, :] = jnp.where(middle, top, whole[0:HALF, :])
        rows[block, HALF:COLS, :] = jnp.where(middle, bottom, whole[HALF:COLS, :])
    for at in range(NP // 2):
        here = slice(at * BLK, (at + 1) * BLK)
        own, other = by_core(rows[2 * at], rows[2 * at + 1])
        parts[0][:, here], parts[1][:, here] = split(own)
        parts[2][:, here], parts[3][:, here] = split(other)
    update = multiply(parts[0], parts[1], own_high, own_low) + multiply(
        parts[2], parts[3], other_high, other_low
    )
    for row in range(COLS):
        out[row, 0:1, :] = child[row, 0:1, :] + update[row:row + 1, :]


def call(kernel, rows, microseconds, *parts):
    return pl.pallas_call(
        kernel,
        out_shape=tuple(jax.ShapeDtypeStruct((count, S1), jnp.float32) for count in rows),
        in_specs=in_vmem(len(parts)),
        out_specs=tuple(in_vmem(len(rows))),
        cost_estimate=hint(microseconds),
        compiler_params=pltpu.CompilerParams(vmem_limit_bytes=VMEM_LIMIT),
    )(*parts)


def shards(ancestor_inverse, pattern, child_lower, child_diag_inv):
    params = pltpu.CompilerParams(vmem_limit_bytes=VMEM_LIMIT)
    own = child_lower[0]
    spread = pl.pallas_call(
        spread_kernel,
        out_shape=jax.ShapeDtypeStruct((N_LEAF, PIECE1, BLK), jnp.float32),
        in_specs=[pl.BlockSpec(memory_space=pl.ANY)] * 2,
        out_specs=in_vmem(1)[0],
        scratch_shapes=[
            pltpu.VMEM((ROWS, OWN_BLOCKS * BLK), jnp.float32),
            pltpu.VMEM((1, NP), jnp.int32),
            pltpu.SemaphoreType.DMA((2,)),
        ],
        compiler_params=pltpu.CompilerParams(vmem_limit_bytes=SPREAD_LIMIT),
    )(ancestor_inverse, pattern)
    across = swap_side(own)
    pair = pl.pallas_call(
        pair_kernel,
        out_shape=jax.ShapeDtypeStruct((64, S1), jnp.float32),
        in_specs=in_vmem(2),
        out_specs=in_vmem(1)[0],
        cost_estimate=hint(2000),
        compiler_params=params,
    )(own, across)
    ahead, behind = from_row(pair, 2), from_row(pair, -2)
    spread = lax.all_to_all(spread, "leaf", 0, 0, tiled=True)
    chosen = pl.pallas_call(
        select_kernel,
        out_shape=jax.ShapeDtypeStruct((N_LEAF, PIECE2, BLK), jnp.float32),
        in_specs=[pl.BlockSpec(memory_space=pl.ANY)],
        out_specs=pl.BlockSpec(memory_space=pl.ANY),
        scratch_shapes=[
            pltpu.VMEM((N_LEAF, PIECE1, BLK), jnp.float32),
            pltpu.VMEM((N_LEAF, PIECE2, BLK), jnp.float32),
            pltpu.SMEM((N_LEAF, 1, BLK), jnp.float32),
            pltpu.SemaphoreType.DMA((2 + SELECT_PARTS,)),
        ],
        compiler_params=params,
    )(spread)
    chosen = lax.all_to_all(chosen, "leaf", 0, 0, tiled=True)
    near, rear = call(near_kernel, (192, 64), 2000, pair, ahead, behind)
    (lower,) = call(
        join_kernel,
        (NP * 64,),
        0,
        near,
        from_row(near, 1),
        from_row(rear, -1),
        from_row(rear, -2),
    )
    lower, chosen = lax.optimization_barrier((lower, chosen))
    lower_other = lax.ppermute(lower, "core", [(0, 1), (1, 0)])
    lower_shape = jax.ShapeDtypeStruct((NP * 64, S1), jnp.bfloat16)
    panel_shape = jax.ShapeDtypeStruct((ROWS, NP * 64), jnp.bfloat16)
    partial, panel_high, panel_low, own_high, own_low = pl.pallas_call(
        own_kernel,
        out_shape=(
            jax.ShapeDtypeStruct((ROWS, S1), jnp.float32),
            panel_shape,
            panel_shape,
            lower_shape,
            lower_shape,
        ),
        in_specs=in_vmem(2),
        out_specs=tuple(in_vmem(5)),
        scratch_shapes=[
            pltpu.VMEM((ROWS, NP * BLK), jnp.float32),
            pltpu.VMEM((ROWS, NP * 64), jnp.bfloat16),
            pltpu.VMEM((ROWS, NP * 64), jnp.bfloat16),
        ],
        compiler_params=params,
    )(chosen, lower)
    cross, pieces, other_high, other_low = pl.pallas_call(
        cross_kernel,
        out_shape=(
            jax.ShapeDtypeStruct((1, ROWS, S1), jnp.float32),
            jax.ShapeDtypeStruct((N_GRID * PIECE3, BLK), jnp.float32),
            lower_shape,
            lower_shape,
        ),
        in_specs=in_vmem(4),
        out_specs=tuple(in_vmem(4)),
        scratch_shapes=[pltpu.VMEM((ROWS, S1), jnp.float32)],
        compiler_params=params,
    )(partial, panel_high, panel_low, lower_other)
    pieces = lax.all_to_all(
        pieces.reshape(N_GRID, PIECE3, 1, BLK), GRID, 0, 0, tiled=True
    ).reshape(N_GRID * PIECE3, BLK)
    diagonal = pl.pallas_call(
        diagonal_kernel,
        out_shape=jax.ShapeDtypeStruct((COLS, 1, S1), jnp.float32),
        in_specs=[pl.BlockSpec(memory_space=pltpu.SMEM)] + in_vmem(6),
        out_specs=in_vmem(1)[0],
        scratch_shapes=[pltpu.VMEM((NP, 32, BLK), jnp.float32)]
        + [pltpu.VMEM((32, NP * 64), jnp.bfloat16)] * 4,
        compiler_params=params,
    )(
        pattern,
        pieces,
        own_high,
        own_low,
        other_high,
        other_low,
        jnp.transpose(child_diag_inv, (1, 0, 2)),
    )
    return cross, jnp.transpose(diagonal, (1, 0, 2))


def solution(mesh):
    shape = mesh.shape
    parts = Mesh(
        mesh.devices.reshape(shape["leaf"], shape["prow"], shape["pcol"] // 2, 2), ("leaf",) + GRID
    )
    return jax.shard_map(
        shards,
        mesh=parts,
        in_specs=(
            P(GRID, "leaf"),
            P("leaf", None),
            P("leaf", GRID, None),
            P("leaf", GRID, None),
        ),
        out_specs=(P("leaf", GRID, None), P("leaf", GRID, None)),
        check_vma=False,
    )
```

```python
import jax
import jax.numpy as jnp
from jax import lax
from jax.experimental import pallas as pl
from jax.experimental.pallas import tpu as pltpu
from jax.sharding import Mesh
from jax.sharding import PartitionSpec as P

BLK = 128
NP = 8
N_LEAF = 16
N_GRID = 32
ROWS = 192
CHUNK = ROWS // N_LEAF
OWN_BLOCKS = 3
S1 = 896
COLS = S1 // N_GRID
LROWS = 32
SELECT_PARTS = 4
PAT_ROW = OWN_BLOCKS * CHUNK
PIECE1 = 40
PIECE2 = NP * CHUNK
HALF = COLS // 2
PIECE3 = COLS + HALF
VMEM_LIMIT = 16 * 1024 * 1024
SPREAD_LIMIT = 63 * 1024 * 1024


GRID = ("prow", "side", "core")


STEPS = (0, 2, -2, 1, 3, -1, -3, 4)


def from_row(value, distance):
    return lax.ppermute(value, "prow", [(at, (at - distance) % NP) for at in range(NP)])


def swap_side(value):
    return lax.ppermute(value, "side", [(0, 1), (1, 0)])


def hint(microseconds):
    return pl.CostEstimate(flops=int(microseconds * 1.1e9), bytes_accessed=int(microseconds * 3.7e6), transcendentals=0)


def in_vmem(count):
    return [pl.BlockSpec(memory_space=pltpu.VMEM)] * count


def split(value):
    high = value.astype(jnp.bfloat16)
    low = (value - high.astype(jnp.float32)).astype(jnp.bfloat16)
    return high, low


def spread_kernel(ancestor, pattern, out, panel, numbers, semaphores):
    copies = [
        pltpu.make_async_copy(ancestor, panel, semaphores.at[0]),
        pltpu.make_async_copy(pattern, numbers, semaphores.at[1]),
    ]
    for copy in copies:
        copy.start()
    for copy in copies:
        copy.wait()
    row = numbers[...].astype(jnp.float32)
    for leaf in range(N_LEAF):
        for block in range(OWN_BLOCKS):
            out[leaf, block * CHUNK:(block + 1) * CHUNK, :] = panel[
                leaf * CHUNK:(leaf + 1) * CHUNK, block * BLK:(block + 1) * BLK
            ]
        out[leaf, PAT_ROW:PIECE1, :] = jnp.zeros((PIECE1 - PAT_ROW, BLK), jnp.float32)
        out[leaf, PAT_ROW:PAT_ROW + 1, 0:NP] = row


def pair_kernel(own, across, out):
    out[0:LROWS, :] = own[...]
    out[LROWS:2 * LROWS, :] = across[...]


def stack(out, *parts):
    first = 0
    for part in parts:
        rows = part.shape[0]
        out[first:first + rows, :] = part[...]
        first += rows


def near_kernel(pair, ahead, behind, near, rear):
    stack(near, pair, ahead, behind)
    rear[...] = behind[...]


def join_kernel(*refs):
    stack(refs[-1], *refs[:-1])


def select_kernel(pieces, out, held, chosen, patterns, semaphores):
    copies = [
        pltpu.make_async_copy(pieces, held, semaphores.at[0]),
        pltpu.make_async_copy(pieces.at[:, PAT_ROW:PAT_ROW + 1, :], patterns, semaphores.at[1]),
    ]
    for copy in copies:
        copy.start()
    for copy in copies:
        copy.wait()
    sent = []
    for part in range(SELECT_PARTS):
        count = N_LEAF // SELECT_PARTS
        for leaf in range(part * count, (part + 1) * count):
            for block in range(NP):
                number = patterns[leaf, 0, block].astype(jnp.int32)
                owner = number // OWN_BLOCKS
                first = (number - owner * OWN_BLOCKS) * CHUNK
                chosen[leaf, block * CHUNK:(block + 1) * CHUNK, :] = held[
                    owner, pl.ds(first, CHUNK), :
                ]
        here = pl.ds(part * count, count)
        sent.append(pltpu.make_async_copy(chosen.at[here], out.at[here], semaphores.at[2 + part]))
        sent[-1].start()
    for copy in sent:
        copy.wait()


def by_core(first, second):
    lane = lax.broadcasted_iota(jnp.int32, first.shape, 1)

    def even(value):
        return jnp.where(lane < 32, value, pltpu.roll(value, 96, 1))

    def odd(value):
        return jnp.where(lane < 32, pltpu.roll(value, 96, 1), pltpu.roll(value, 64, 1))

    cores = [
        jnp.where(lane < 64, pick(first), pltpu.roll(pick(second), 64, 1)) for pick in (even, odd)
    ]
    swap = lax.axis_index("core") == 1
    return jnp.where(swap, cores[1], cores[0]), jnp.where(swap, cores[0], cores[1])


def order_rows(source, high_out, low_out):
    side = lax.axis_index("side")
    place = lax.axis_index("prow")
    for group, step in enumerate(STEPS):
        block = lax.rem(place + step + NP, NP)
        for part, at_side in ((0, side), (1, 1 - side)):
            row = group * 64 + part * LROWS
            high, low = split(source[row:row + LROWS, :])
            first = pl.multiple_of(block * 64 + at_side * LROWS, LROWS)
            high_out[pl.ds(first, LROWS), :] = high
            low_out[pl.ds(first, LROWS), :] = low


def multiply(both, lower_high, lower_low):
    count = both.shape[0] // 2
    first = jnp.dot(both[...], lower_high[...], preferred_element_type=jnp.float32)
    second = jnp.dot(both[0:count, :], lower_low[...], preferred_element_type=jnp.float32)
    return first[0:count, :] + (first[count:, :] + second)


def put_both(out, lanes, value):
    count = value.shape[0]
    out[0:count, lanes], out[count:, lanes] = split(value)


def own_kernel(pieces, lower, partial, other_both, lower_high, lower_low, panel, own_both):
    for leaf in range(N_LEAF):
        for block in range(NP):
            panel[leaf * CHUNK:(leaf + 1) * CHUNK, block * BLK:(block + 1) * BLK] = pieces[
                leaf, block * CHUNK:(block + 1) * CHUNK, :
            ]
    for at in range(NP // 2):
        here = slice(at * BLK, (at + 1) * BLK)
        own, other = by_core(
            panel[:, 2 * at * BLK:(2 * at + 1) * BLK], panel[:, (2 * at + 1) * BLK:(2 * at + 2) * BLK]
        )
        put_both(own_both, here, own)
        put_both(other_both, here, other)
    order_rows(lower, lower_high, lower_low)
    partial[...] = multiply(own_both, lower_high, lower_low)


def cross_kernel(partial, both, lower, cross, out, lower_high, lower_low, product):
    core = lax.axis_index("core")
    order_rows(lower, lower_high, lower_low)
    value = partial[...] + multiply(both, lower_high, lower_low)
    product[...] = value
    cross[0, :, :] = -value
    whole = product[pl.ds(pl.multiple_of(core * 64, 64), BLK), :].T
    half = product[pl.ds(pl.multiple_of((1 - core) * BLK, BLK), 64), :].T
    for device in range(N_GRID):
        at = device * COLS
        first = device * PIECE3
        out[first:first + COLS, :] = whole[at:at + COLS, :]
        out[first + COLS:first + PIECE3, 0:64] = half[at:at + HALF, :]
        out[first + COLS:first + PIECE3, 64:128] = half[at + HALF:at + COLS, :]


def diagonal_kernel(
    pattern, pieces, own_high, own_low, other_high, other_low, child, out, rows, own_both, other_both
):
    lane = lax.broadcasted_iota(jnp.int32, (HALF, BLK), 1)
    rows[:, COLS:, :] = jnp.zeros((NP, 32 - COLS, BLK), jnp.float32)
    for block in range(NP):
        number = pattern[0, block]
        group = number // 3
        place = number - group * 3
        upper = 2 * group
        middle = place == 1
        whole = pieces[pl.ds((upper + place // 2) * PIECE3, COLS), :]
        first = pieces[pl.ds(upper * PIECE3 + COLS - 2, HALF + 2), :][2:, :]
        second = pieces[pl.ds((upper + 1) * PIECE3 + COLS - 2, HALF + 2), :][2:, :]
        top = jnp.where(lane < 64, first, pltpu.roll(second, 64, 1))
        bottom = jnp.where(lane < 64, pltpu.roll(first, 64, 1), second)
        rows[block, 0:HALF, :] = jnp.where(middle, top, whole[0:HALF, :])
        rows[block, HALF:COLS, :] = jnp.where(middle, bottom, whole[HALF:COLS, :])
    for at in range(NP // 2):
        here = slice(at * BLK, (at + 1) * BLK)
        own, other = by_core(rows[2 * at], rows[2 * at + 1])
        put_both(own_both, here, own)
        put_both(other_both, here, other)
    update = multiply(own_both, own_high, own_low) + multiply(other_both, other_high, other_low)
    for row in range(COLS):
        out[row, 0:1, :] = child[row, 0:1, :] + update[row:row + 1, :]


def call(kernel, rows, microseconds, *parts):
    return pl.pallas_call(
        kernel,
        out_shape=tuple(jax.ShapeDtypeStruct((count, S1), jnp.float32) for count in rows),
        in_specs=in_vmem(len(parts)),
        out_specs=tuple(in_vmem(len(rows))),
        cost_estimate=hint(microseconds),
        compiler_params=pltpu.CompilerParams(vmem_limit_bytes=VMEM_LIMIT),
    )(*parts)


def shards(ancestor_inverse, pattern, child_lower, child_diag_inv):
    params = pltpu.CompilerParams(vmem_limit_bytes=VMEM_LIMIT)
    own = child_lower[0]
    spread = pl.pallas_call(
        spread_kernel,
        out_shape=jax.ShapeDtypeStruct((N_LEAF, PIECE1, BLK), jnp.float32),
        in_specs=[pl.BlockSpec(memory_space=pl.ANY)] * 2,
        out_specs=in_vmem(1)[0],
        scratch_shapes=[
            pltpu.VMEM((ROWS, OWN_BLOCKS * BLK), jnp.float32),
            pltpu.VMEM((1, NP), jnp.int32),
            pltpu.SemaphoreType.DMA((2,)),
        ],
        compiler_params=pltpu.CompilerParams(vmem_limit_bytes=SPREAD_LIMIT),
    )(ancestor_inverse, pattern)
    across = swap_side(own)
    pair = pl.pallas_call(
        pair_kernel,
        out_shape=jax.ShapeDtypeStruct((64, S1), jnp.float32),
        in_specs=in_vmem(2),
        out_specs=in_vmem(1)[0],
        cost_estimate=hint(2000),
        compiler_params=params,
    )(own, across)
    ahead, behind = from_row(pair, 2), from_row(pair, -2)
    spread = lax.all_to_all(spread, "leaf", 0, 0, tiled=True)
    chosen = pl.pallas_call(
        select_kernel,
        out_shape=jax.ShapeDtypeStruct((N_LEAF, PIECE2, BLK), jnp.float32),
        in_specs=[pl.BlockSpec(memory_space=pl.ANY)],
        out_specs=pl.BlockSpec(memory_space=pl.ANY),
        scratch_shapes=[
            pltpu.VMEM((N_LEAF, PIECE1, BLK), jnp.float32),
            pltpu.VMEM((N_LEAF, PIECE2, BLK), jnp.float32),
            pltpu.SMEM((N_LEAF, 1, BLK), jnp.float32),
            pltpu.SemaphoreType.DMA((2 + SELECT_PARTS,)),
        ],
        compiler_params=params,
    )(spread)
    chosen = lax.all_to_all(chosen, "leaf", 0, 0, tiled=True)
    near, rear = call(near_kernel, (192, 64), 2000, pair, ahead, behind)
    (lower,) = call(
        join_kernel,
        (NP * 64,),
        0,
        near,
        from_row(near, 1),
        from_row(rear, -1),
        from_row(rear, -2),
    )
    lower, chosen = lax.optimization_barrier((lower, chosen))
    lower_other = lax.ppermute(lower, "core", [(0, 1), (1, 0)])
    lower_shape = jax.ShapeDtypeStruct((NP * 64, S1), jnp.bfloat16)
    panel_shape = jax.ShapeDtypeStruct((2 * ROWS, NP * 64), jnp.bfloat16)
    partial, panel_both, own_high, own_low = pl.pallas_call(
        own_kernel,
        out_shape=(
            jax.ShapeDtypeStruct((ROWS, S1), jnp.float32),
            panel_shape,
            lower_shape,
            lower_shape,
        ),
        in_specs=in_vmem(2),
        out_specs=tuple(in_vmem(4)),
        scratch_shapes=[
            pltpu.VMEM((ROWS, NP * BLK), jnp.float32),
            pltpu.VMEM((2 * ROWS, NP * 64), jnp.bfloat16),
        ],
        compiler_params=params,
    )(chosen, lower)
    cross, pieces, other_high, other_low = pl.pallas_call(
        cross_kernel,
        out_shape=(
            jax.ShapeDtypeStruct((1, ROWS, S1), jnp.float32),
            jax.ShapeDtypeStruct((N_GRID * PIECE3, BLK), jnp.float32),
            lower_shape,
            lower_shape,
        ),
        in_specs=in_vmem(3),
        out_specs=tuple(in_vmem(4)),
        scratch_shapes=[pltpu.VMEM((ROWS, S1), jnp.float32)],
        compiler_params=params,
    )(partial, panel_both, lower_other)
    pieces = lax.all_to_all(
        pieces.reshape(N_GRID, PIECE3, 1, BLK), GRID, 0, 0, tiled=True
    ).reshape(N_GRID * PIECE3, BLK)
    diagonal = pl.pallas_call(
        diagonal_kernel,
        out_shape=jax.ShapeDtypeStruct((COLS, 1, S1), jnp.float32),
        in_specs=[pl.BlockSpec(memory_space=pltpu.SMEM)] + in_vmem(6),
        out_specs=in_vmem(1)[0],
        scratch_shapes=[pltpu.VMEM((NP, 32, BLK), jnp.float32)]
        + [pltpu.VMEM((64, NP * 64), jnp.bfloat16)] * 2,
        compiler_params=params,
    )(
        pattern,
        pieces,
        own_high,
        own_low,
        other_high,
        other_low,
        jnp.transpose(child_diag_inv, (1, 0, 2)),
    )
    return cross, jnp.transpose(diagonal, (1, 0, 2))


def solution(mesh):
    shape = mesh.shape
    parts = Mesh(
        mesh.devices.reshape(shape["leaf"], shape["prow"], shape["pcol"] // 2, 2), ("leaf",) + GRID
    )
    return jax.shard_map(
        shards,
        mesh=parts,
        in_specs=(
            P(GRID, "leaf"),
            P("leaf", None),
            P("leaf", GRID, None),
            P("leaf", GRID, None),
        ),
        out_specs=(P("leaf", GRID, None), P("leaf", GRID, None)),
        check_vma=False,
    )
```

```python
import jax
import jax.numpy as jnp
from jax import lax
from jax.experimental import pallas as pl
from jax.experimental.pallas import tpu as pltpu
from jax.sharding import Mesh
from jax.sharding import PartitionSpec as P

BLK = 128
NP = 8
N_LEAF = 16
N_GRID = 32
ROWS = 192
CHUNK = ROWS // N_LEAF
OWN_BLOCKS = 3
S1 = 896
COLS = S1 // N_GRID
LROWS = 32
SELECT_PARTS = 4
PAT_ROW = OWN_BLOCKS * CHUNK
PIECE1 = 40
PIECE2 = NP * CHUNK
HALF = COLS // 2
PIECE3 = COLS + HALF
VMEM_LIMIT = 16 * 1024 * 1024
SPREAD_LIMIT = 63 * 1024 * 1024


GRID = ("prow", "side", "core")


STEPS = (0, 2, -2, 1, 3, -1, -3, 4)


def from_row(value, distance):
    return lax.ppermute(value, "prow", [(at, (at - distance) % NP) for at in range(NP)])


def swap_core(value):
    return lax.ppermute(value, "core", [(0, 1), (1, 0)])


def swap_side(value):
    return lax.ppermute(value, "side", [(0, 1), (1, 0)])


def hint(microseconds):
    return pl.CostEstimate(flops=int(microseconds * 1.1e9), bytes_accessed=int(microseconds * 3.7e6), transcendentals=0)


def in_vmem(count):
    return [pl.BlockSpec(memory_space=pltpu.VMEM)] * count


def split(value):
    high = value.astype(jnp.bfloat16)
    low = (value - high.astype(jnp.float32)).astype(jnp.bfloat16)
    return high, low


def spread_kernel(ancestor, pattern, out, panel, numbers, semaphores):
    copies = [
        pltpu.make_async_copy(ancestor, panel, semaphores.at[0]),
        pltpu.make_async_copy(pattern, numbers, semaphores.at[1]),
    ]
    for copy in copies:
        copy.start()
    for copy in copies:
        copy.wait()
    row = numbers[...].astype(jnp.float32)
    for leaf in range(N_LEAF):
        for block in range(OWN_BLOCKS):
            out[leaf, block * CHUNK:(block + 1) * CHUNK, :] = panel[
                leaf * CHUNK:(leaf + 1) * CHUNK, block * BLK:(block + 1) * BLK
            ]
        out[leaf, PAT_ROW:PIECE1, :] = jnp.zeros((PIECE1 - PAT_ROW, BLK), jnp.float32)
        out[leaf, PAT_ROW:PAT_ROW + 1, 0:NP] = row


def pair_kernel(own, across, out):
    out[0:LROWS, :] = own[...]
    out[LROWS:2 * LROWS, :] = across[...]


def stack(out, *parts):
    first = 0
    for part in parts:
        rows = part.shape[0]
        out[first:first + rows, :] = part[...]
        first += rows


def near_kernel(pair, ahead, behind, near, rear):
    stack(near, pair, ahead, behind)
    rear[...] = behind[...]


def join_kernel(*refs):
    stack(refs[-1], *refs[:-1])


def select_kernel(pieces, out, held, chosen, patterns, semaphores):
    copies = [
        pltpu.make_async_copy(pieces, held, semaphores.at[0]),
        pltpu.make_async_copy(pieces.at[:, PAT_ROW:PAT_ROW + 1, :], patterns, semaphores.at[1]),
    ]
    for copy in copies:
        copy.start()
    for copy in copies:
        copy.wait()
    sent = []
    for part in range(SELECT_PARTS):
        count = N_LEAF // SELECT_PARTS
        for leaf in range(part * count, (part + 1) * count):
            for block in range(NP):
                number = patterns[leaf, 0, block].astype(jnp.int32)
                owner = number // OWN_BLOCKS
                first = (number - owner * OWN_BLOCKS) * CHUNK
                chosen[leaf, block * CHUNK:(block + 1) * CHUNK, :] = held[
                    owner, pl.ds(first, CHUNK), :
                ]
        here = pl.ds(part * count, count)
        sent.append(pltpu.make_async_copy(chosen.at[here], out.at[here], semaphores.at[2 + part]))
        sent[-1].start()
    for copy in sent:
        copy.wait()


def by_core(first, second):
    lane = lax.broadcasted_iota(jnp.int32, first.shape, 1)

    def even(value):
        return jnp.where(lane < 32, value, pltpu.roll(value, 96, 1))

    def odd(value):
        return jnp.where(lane < 32, pltpu.roll(value, 96, 1), pltpu.roll(value, 64, 1))

    cores = [
        jnp.where(lane < 64, pick(first), pltpu.roll(pick(second), 64, 1)) for pick in (even, odd)
    ]
    swap = lax.axis_index("core") == 1
    return jnp.where(swap, cores[1], cores[0]), jnp.where(swap, cores[0], cores[1])


def order_rows(sources, high_out, low_out):
    side = lax.axis_index("side")
    place = lax.axis_index("prow")
    for index, step in enumerate(STEPS):
        source, group = (sources[index], 0) if index < 3 else (sources[3], index - 3)
        block = lax.rem(place + step + NP, NP)
        for part, at_side in ((0, side), (1, 1 - side)):
            row = group * 64 + part * LROWS
            high, low = split(source[row:row + LROWS, :])
            first = pl.multiple_of(block * 64 + at_side * LROWS, LROWS)
            high_out[pl.ds(first, LROWS), :] = high
            low_out[pl.ds(first, LROWS), :] = low


def multiply(both, lower_high, lower_low):
    count = both.shape[0] // 2
    first = jnp.dot(both[...], lower_high[...], preferred_element_type=jnp.float32)
    second = jnp.dot(both[0:count, :], lower_low[...], preferred_element_type=jnp.float32)
    return first[0:count, :] + (first[count:, :] + second)


def put_both(out, lanes, value):
    count = value.shape[0]
    out[0:count, lanes], out[count:, lanes] = split(value)


def own_kernel(pieces, *refs):
    sources = refs[:4]
    partial, other_both, lower_high, lower_low, panel, own_both = refs[4:]
    for leaf in range(N_LEAF):
        for block in range(NP):
            panel[leaf * CHUNK:(leaf + 1) * CHUNK, block * BLK:(block + 1) * BLK] = pieces[
                leaf, block * CHUNK:(block + 1) * CHUNK, :
            ]
    for at in range(NP // 2):
        here = slice(at * BLK, (at + 1) * BLK)
        own, other = by_core(
            panel[:, 2 * at * BLK:(2 * at + 1) * BLK], panel[:, (2 * at + 1) * BLK:(2 * at + 2) * BLK]
        )
        put_both(own_both, here, own)
        put_both(other_both, here, other)
    order_rows(sources, lower_high, lower_low)
    partial[...] = multiply(own_both, lower_high, lower_low)


def cross_kernel(partial, both, *refs):
    sources = refs[:4]
    cross, out, lower_high, lower_low, product = refs[4:]
    core = lax.axis_index("core")
    order_rows(sources, lower_high, lower_low)
    value = partial[...] + multiply(both, lower_high, lower_low)
    product[...] = value
    cross[0, :, :] = -value
    whole = product[pl.ds(pl.multiple_of(core * 64, 64), BLK), :].T
    half = product[pl.ds(pl.multiple_of((1 - core) * BLK, BLK), 64), :].T
    for device in range(N_GRID):
        at = device * COLS
        first = device * PIECE3
        out[first:first + COLS, :] = whole[at:at + COLS, :]
        out[first + COLS:first + PIECE3, 0:64] = half[at:at + HALF, :]
        out[first + COLS:first + PIECE3, 64:128] = half[at + HALF:at + COLS, :]


def diagonal_kernel(
    pattern, pieces, own_high, own_low, other_high, other_low, child, out, rows, own_both, other_both
):
    lane = lax.broadcasted_iota(jnp.int32, (HALF, BLK), 1)
    rows[:, COLS:, :] = jnp.zeros((NP, 32 - COLS, BLK), jnp.float32)
    for block in range(NP):
        number = pattern[0, block]
        group = number // 3
        place = number - group * 3
        upper = 2 * group
        middle = place == 1
        whole = pieces[pl.ds((upper + place // 2) * PIECE3, COLS), :]
        first = pieces[pl.ds(upper * PIECE3 + COLS - 2, HALF + 2), :][2:, :]
        second = pieces[pl.ds((upper + 1) * PIECE3 + COLS - 2, HALF + 2), :][2:, :]
        top = jnp.where(lane < 64, first, pltpu.roll(second, 64, 1))
        bottom = jnp.where(lane < 64, pltpu.roll(first, 64, 1), second)
        rows[block, 0:HALF, :] = jnp.where(middle, top, whole[0:HALF, :])
        rows[block, HALF:COLS, :] = jnp.where(middle, bottom, whole[HALF:COLS, :])
    for at in range(NP // 2):
        here = slice(at * BLK, (at + 1) * BLK)
        own, other = by_core(rows[2 * at], rows[2 * at + 1])
        put_both(own_both, here, own)
        put_both(other_both, here, other)
    update = multiply(own_both, own_high, own_low) + multiply(other_both, other_high, other_low)
    for row in range(COLS):
        out[row, 0:1, :] = child[row, 0:1, :] + update[row:row + 1, :]


def call(kernel, rows, microseconds, *parts):
    return pl.pallas_call(
        kernel,
        out_shape=tuple(jax.ShapeDtypeStruct((count, S1), jnp.float32) for count in rows),
        in_specs=in_vmem(len(parts)),
        out_specs=tuple(in_vmem(len(rows))),
        cost_estimate=hint(microseconds),
        compiler_params=pltpu.CompilerParams(vmem_limit_bytes=VMEM_LIMIT),
    )(*parts)


def shards(ancestor_inverse, pattern, child_lower, child_diag_inv):
    params = pltpu.CompilerParams(vmem_limit_bytes=VMEM_LIMIT)
    own = child_lower[0]
    spread = pl.pallas_call(
        spread_kernel,
        out_shape=jax.ShapeDtypeStruct((N_LEAF, PIECE1, BLK), jnp.float32),
        in_specs=[pl.BlockSpec(memory_space=pl.ANY)] * 2,
        out_specs=in_vmem(1)[0],
        scratch_shapes=[
            pltpu.VMEM((ROWS, OWN_BLOCKS * BLK), jnp.float32),
            pltpu.VMEM((1, NP), jnp.int32),
            pltpu.SemaphoreType.DMA((2,)),
        ],
        compiler_params=pltpu.CompilerParams(vmem_limit_bytes=SPREAD_LIMIT),
    )(ancestor_inverse, pattern)
    across = swap_side(own)
    pair = pl.pallas_call(
        pair_kernel,
        out_shape=jax.ShapeDtypeStruct((64, S1), jnp.float32),
        in_specs=in_vmem(2),
        out_specs=in_vmem(1)[0],
        cost_estimate=hint(2000),
        compiler_params=params,
    )(own, across)
    ahead, behind = from_row(pair, 2), from_row(pair, -2)
    spread = lax.all_to_all(spread, "leaf", 0, 0, tiled=True)
    chosen = pl.pallas_call(
        select_kernel,
        out_shape=jax.ShapeDtypeStruct((N_LEAF, PIECE2, BLK), jnp.float32),
        in_specs=[pl.BlockSpec(memory_space=pl.ANY)],
        out_specs=pl.BlockSpec(memory_space=pl.ANY),
        scratch_shapes=[
            pltpu.VMEM((N_LEAF, PIECE1, BLK), jnp.float32),
            pltpu.VMEM((N_LEAF, PIECE2, BLK), jnp.float32),
            pltpu.SMEM((N_LEAF, 1, BLK), jnp.float32),
            pltpu.SemaphoreType.DMA((2 + SELECT_PARTS,)),
        ],
        compiler_params=params,
    )(spread)
    chosen = lax.all_to_all(chosen, "leaf", 0, 0, tiled=True)
    near, rear = call(near_kernel, (192, 64), 2000, pair, ahead, behind)
    (far,) = call(
        join_kernel, (320,), 0, from_row(near, 1), from_row(rear, -1), from_row(rear, -2)
    )
    near_parts = [pair, ahead, rear]
    near_other = [swap_core(part) for part in near_parts]
    near_other, far, chosen = lax.optimization_barrier((near_other, far, chosen))
    far_other = swap_core(far)
    lower_shape = jax.ShapeDtypeStruct((NP * 64, S1), jnp.bfloat16)
    panel_shape = jax.ShapeDtypeStruct((2 * ROWS, NP * 64), jnp.bfloat16)
    partial, panel_both, own_high, own_low = pl.pallas_call(
        own_kernel,
        out_shape=(
            jax.ShapeDtypeStruct((ROWS, S1), jnp.float32),
            panel_shape,
            lower_shape,
            lower_shape,
        ),
        in_specs=in_vmem(5),
        out_specs=tuple(in_vmem(4)),
        scratch_shapes=[
            pltpu.VMEM((ROWS, NP * BLK), jnp.float32),
            pltpu.VMEM((2 * ROWS, NP * 64), jnp.bfloat16),
        ],
        compiler_params=params,
    )(chosen, *near_parts, far)
    cross, pieces, other_high, other_low = pl.pallas_call(
        cross_kernel,
        out_shape=(
            jax.ShapeDtypeStruct((1, ROWS, S1), jnp.float32),
            jax.ShapeDtypeStruct((N_GRID * PIECE3, BLK), jnp.float32),
            lower_shape,
            lower_shape,
        ),
        in_specs=in_vmem(6),
        out_specs=tuple(in_vmem(4)),
        scratch_shapes=[pltpu.VMEM((ROWS, S1), jnp.float32)],
        compiler_params=params,
    )(partial, panel_both, *near_other, far_other)
    pieces = lax.all_to_all(
        pieces.reshape(N_GRID, PIECE3, 1, BLK), GRID, 0, 0, tiled=True
    ).reshape(N_GRID * PIECE3, BLK)
    diagonal = pl.pallas_call(
        diagonal_kernel,
        out_shape=jax.ShapeDtypeStruct((COLS, 1, S1), jnp.float32),
        in_specs=[pl.BlockSpec(memory_space=pltpu.SMEM)] + in_vmem(6),
        out_specs=in_vmem(1)[0],
        scratch_shapes=[pltpu.VMEM((NP, 32, BLK), jnp.float32)]
        + [pltpu.VMEM((64, NP * 64), jnp.bfloat16)] * 2,
        compiler_params=params,
    )(
        pattern,
        pieces,
        own_high,
        own_low,
        other_high,
        other_low,
        jnp.transpose(child_diag_inv, (1, 0, 2)),
    )
    return cross, jnp.transpose(diagonal, (1, 0, 2))


def solution(mesh):
    shape = mesh.shape
    parts = Mesh(
        mesh.devices.reshape(shape["leaf"], shape["prow"], shape["pcol"] // 2, 2), ("leaf",) + GRID
    )
    return jax.shard_map(
        shards,
        mesh=parts,
        in_specs=(
            P(GRID, "leaf"),
            P("leaf", None),
            P("leaf", GRID, None),
            P("leaf", GRID, None),
        ),
        out_specs=(P("leaf", GRID, None), P("leaf", GRID, None)),
        check_vma=False,
    )
```

```python
import jax
import jax.numpy as jnp
from jax import lax
from jax.experimental import pallas as pl
from jax.experimental.pallas import tpu as pltpu
from jax.sharding import Mesh
from jax.sharding import PartitionSpec as P

BLK = 128
NP = 8
N_LEAF = 16
N_GRID = 32
ROWS = 192
CHUNK = ROWS // N_LEAF
OWN_BLOCKS = 3
S1 = 896
COLS = S1 // N_GRID
LROWS = 32
SELECT_PARTS = 4
PAT_ROW = OWN_BLOCKS * CHUNK
PIECE1 = 40
PIECE2 = NP * CHUNK
HALF = COLS // 2
PIECE3 = COLS + HALF
VMEM_LIMIT = 16 * 1024 * 1024
SPREAD_LIMIT = 63 * 1024 * 1024


GRID = ("prow", "side", "core")


STEPS = (0, 2, -2, 1, 3, -1, -3, 4)


def from_row(value, distance):
    return lax.ppermute(value, "prow", [(at, (at - distance) % NP) for at in range(NP)])


def swap_core(value):
    return lax.ppermute(value, "core", [(0, 1), (1, 0)])


def swap_side(value):
    return lax.ppermute(value, "side", [(0, 1), (1, 0)])


def hint(microseconds):
    return pl.CostEstimate(flops=int(microseconds * 1.1e9), bytes_accessed=int(microseconds * 3.7e6), transcendentals=0)


def in_vmem(count):
    return [pl.BlockSpec(memory_space=pltpu.VMEM)] * count


def split(value):
    high = value.astype(jnp.bfloat16)
    low = (value - high.astype(jnp.float32)).astype(jnp.bfloat16)
    return high, low


def spread_kernel(ancestor, pattern, out, panel, numbers, semaphores):
    copies = [
        pltpu.make_async_copy(ancestor, panel, semaphores.at[0]),
        pltpu.make_async_copy(pattern, numbers, semaphores.at[1]),
    ]
    for copy in copies:
        copy.start()
    for copy in copies:
        copy.wait()
    row = numbers[...].astype(jnp.float32)
    for leaf in range(N_LEAF):
        for block in range(OWN_BLOCKS):
            out[leaf, block * CHUNK:(block + 1) * CHUNK, :] = panel[
                leaf * CHUNK:(leaf + 1) * CHUNK, block * BLK:(block + 1) * BLK
            ]
        out[leaf, PAT_ROW:PIECE1, :] = jnp.zeros((PIECE1 - PAT_ROW, BLK), jnp.float32)
        out[leaf, PAT_ROW:PAT_ROW + 1, 0:NP] = row


def pair_kernel(own, across, out):
    out[0:LROWS, :] = own[...]
    out[LROWS:2 * LROWS, :] = across[...]


def stack(out, *parts):
    first = 0
    for part in parts:
        rows = part.shape[0]
        out[first:first + rows, :] = part[...]
        first += rows


def near_kernel(pair, ahead, behind, near, rear):
    stack(near, pair, ahead, behind)
    rear[...] = behind[...]


def join_kernel(*refs):
    stack(refs[-1], *refs[:-1])


def select_kernel(pieces, out, held, chosen, patterns, semaphores):
    copies = [
        pltpu.make_async_copy(pieces, held, semaphores.at[0]),
        pltpu.make_async_copy(pieces.at[:, PAT_ROW:PAT_ROW + 1, :], patterns, semaphores.at[1]),
    ]
    for copy in copies:
        copy.start()
    for copy in copies:
        copy.wait()
    sent = []
    for part in range(SELECT_PARTS):
        count = N_LEAF // SELECT_PARTS
        for leaf in range(part * count, (part + 1) * count):
            for block in range(NP):
                number = patterns[leaf, 0, block].astype(jnp.int32)
                owner = number // OWN_BLOCKS
                first = (number - owner * OWN_BLOCKS) * CHUNK
                chosen[leaf, block * CHUNK:(block + 1) * CHUNK, :] = held[
                    owner, pl.ds(first, CHUNK), :
                ]
        here = pl.ds(part * count, count)
        sent.append(pltpu.make_async_copy(chosen.at[here], out.at[here], semaphores.at[2 + part]))
        sent[-1].start()
    for copy in sent:
        copy.wait()


def by_core(first, second):
    lane = lax.broadcasted_iota(jnp.int32, first.shape, 1)

    def even(value):
        return jnp.where(lane < 32, value, pltpu.roll(value, 96, 1))

    def odd(value):
        return jnp.where(lane < 32, pltpu.roll(value, 96, 1), pltpu.roll(value, 64, 1))

    cores = [
        jnp.where(lane < 64, pick(first), pltpu.roll(pick(second), 64, 1)) for pick in (even, odd)
    ]
    swap = lax.axis_index("core") == 1
    return jnp.where(swap, cores[1], cores[0]), jnp.where(swap, cores[0], cores[1])


def order_rows(sources, high_out, low_out):
    side = lax.axis_index("side")
    place = lax.axis_index("prow")
    for index, step in enumerate(STEPS):
        source, group = (sources[index], 0) if index < 2 else (sources[2], index - 2)
        block = lax.rem(place + step + NP, NP)
        for part, at_side in ((0, side), (1, 1 - side)):
            row = group * 64 + part * LROWS
            high, low = split(source[row:row + LROWS, :])
            first = pl.multiple_of(block * 64 + at_side * LROWS, LROWS)
            high_out[pl.ds(first, LROWS), :] = high
            low_out[pl.ds(first, LROWS), :] = low


def multiply(both, lower_high, lower_low):
    count = both.shape[0] // 2
    first = jnp.dot(both[...], lower_high[...], preferred_element_type=jnp.float32)
    second = jnp.dot(both[0:count, :], lower_low[...], preferred_element_type=jnp.float32)
    return first[0:count, :] + (first[count:, :] + second)


def put_both(out, lanes, value):
    count = value.shape[0]
    out[0:count, lanes], out[count:, lanes] = split(value)


def own_kernel(pieces, *refs):
    sources = refs[:3]
    partial, other_both, lower_high, lower_low, panel, own_both = refs[3:]
    for leaf in range(N_LEAF):
        for block in range(NP):
            panel[leaf * CHUNK:(leaf + 1) * CHUNK, block * BLK:(block + 1) * BLK] = pieces[
                leaf, block * CHUNK:(block + 1) * CHUNK, :
            ]
    for at in range(NP // 2):
        here = slice(at * BLK, (at + 1) * BLK)
        own, other = by_core(
            panel[:, 2 * at * BLK:(2 * at + 1) * BLK], panel[:, (2 * at + 1) * BLK:(2 * at + 2) * BLK]
        )
        put_both(own_both, here, own)
        put_both(other_both, here, other)
    order_rows(sources, lower_high, lower_low)
    partial[...] = multiply(own_both, lower_high, lower_low)


def cross_kernel(partial, both, *refs):
    sources = refs[:3]
    cross, out, lower_high, lower_low, product = refs[3:]
    core = lax.axis_index("core")
    order_rows(sources, lower_high, lower_low)
    value = partial[...] + multiply(both, lower_high, lower_low)
    product[...] = value
    cross[0, :, :] = -value
    whole = product[pl.ds(pl.multiple_of(core * 64, 64), BLK), :].T
    half = product[pl.ds(pl.multiple_of((1 - core) * BLK, BLK), 64), :].T
    for device in range(N_GRID):
        at = device * COLS
        first = device * PIECE3
        out[first:first + COLS, :] = whole[at:at + COLS, :]
        out[first + COLS:first + PIECE3, 0:64] = half[at:at + HALF, :]
        out[first + COLS:first + PIECE3, 64:128] = half[at + HALF:at + COLS, :]


def diagonal_kernel(
    pattern, pieces, own_high, own_low, other_high, other_low, child, out, rows, own_both, other_both
):
    lane = lax.broadcasted_iota(jnp.int32, (HALF, BLK), 1)
    rows[:, COLS:, :] = jnp.zeros((NP, 32 - COLS, BLK), jnp.float32)
    for block in range(NP):
        number = pattern[0, block]
        group = number // 3
        place = number - group * 3
        upper = 2 * group
        middle = place == 1
        whole = pieces[pl.ds((upper + place // 2) * PIECE3, COLS), :]
        first = pieces[pl.ds(upper * PIECE3 + COLS - 2, HALF + 2), :][2:, :]
        second = pieces[pl.ds((upper + 1) * PIECE3 + COLS - 2, HALF + 2), :][2:, :]
        top = jnp.where(lane < 64, first, pltpu.roll(second, 64, 1))
        bottom = jnp.where(lane < 64, pltpu.roll(first, 64, 1), second)
        rows[block, 0:HALF, :] = jnp.where(middle, top, whole[0:HALF, :])
        rows[block, HALF:COLS, :] = jnp.where(middle, bottom, whole[HALF:COLS, :])
    for at in range(NP // 2):
        here = slice(at * BLK, (at + 1) * BLK)
        own, other = by_core(rows[2 * at], rows[2 * at + 1])
        put_both(own_both, here, own)
        put_both(other_both, here, other)
    update = multiply(own_both, own_high, own_low) + multiply(other_both, other_high, other_low)
    for row in range(COLS):
        out[row, 0:1, :] = child[row, 0:1, :] + update[row:row + 1, :]


def call(kernel, rows, microseconds, *parts):
    return pl.pallas_call(
        kernel,
        out_shape=tuple(jax.ShapeDtypeStruct((count, S1), jnp.float32) for count in rows),
        in_specs=in_vmem(len(parts)),
        out_specs=tuple(in_vmem(len(rows))),
        cost_estimate=hint(microseconds),
        compiler_params=pltpu.CompilerParams(vmem_limit_bytes=VMEM_LIMIT),
    )(*parts)


def shards(ancestor_inverse, pattern, child_lower, child_diag_inv):
    params = pltpu.CompilerParams(vmem_limit_bytes=VMEM_LIMIT)
    own = child_lower[0]
    spread = pl.pallas_call(
        spread_kernel,
        out_shape=jax.ShapeDtypeStruct((N_LEAF, PIECE1, BLK), jnp.float32),
        in_specs=[pl.BlockSpec(memory_space=pl.ANY)] * 2,
        out_specs=in_vmem(1)[0],
        scratch_shapes=[
            pltpu.VMEM((ROWS, OWN_BLOCKS * BLK), jnp.float32),
            pltpu.VMEM((1, NP), jnp.int32),
            pltpu.SemaphoreType.DMA((2,)),
        ],
        compiler_params=pltpu.CompilerParams(vmem_limit_bytes=SPREAD_LIMIT),
    )(ancestor_inverse, pattern)
    across = swap_side(own)
    pair = pl.pallas_call(
        pair_kernel,
        out_shape=jax.ShapeDtypeStruct((64, S1), jnp.float32),
        in_specs=in_vmem(2),
        out_specs=in_vmem(1)[0],
        cost_estimate=hint(2000),
        compiler_params=params,
    )(own, across)
    ahead, behind = from_row(pair, 2), from_row(pair, -2)
    spread = lax.all_to_all(spread, "leaf", 0, 0, tiled=True)
    chosen = pl.pallas_call(
        select_kernel,
        out_shape=jax.ShapeDtypeStruct((N_LEAF, PIECE2, BLK), jnp.float32),
        in_specs=[pl.BlockSpec(memory_space=pl.ANY)],
        out_specs=pl.BlockSpec(memory_space=pl.ANY),
        scratch_shapes=[
            pltpu.VMEM((N_LEAF, PIECE1, BLK), jnp.float32),
            pltpu.VMEM((N_LEAF, PIECE2, BLK), jnp.float32),
            pltpu.SMEM((N_LEAF, 1, BLK), jnp.float32),
            pltpu.SemaphoreType.DMA((2 + SELECT_PARTS,)),
        ],
        compiler_params=params,
    )(spread)
    chosen = lax.all_to_all(chosen, "leaf", 0, 0, tiled=True)
    near, rear = call(near_kernel, (192, 64), 2000, pair, ahead, behind)
    (far,) = call(
        join_kernel, (384,), 0, rear, from_row(near, 1), from_row(rear, -1), from_row(rear, -2)
    )
    near_parts = [pair, ahead]
    near_other = [swap_core(part) for part in near_parts]
    near_other, far, chosen = lax.optimization_barrier((near_other, far, chosen))
    far_other = swap_core(far)
    lower_shape = jax.ShapeDtypeStruct((NP * 64, S1), jnp.bfloat16)
    panel_shape = jax.ShapeDtypeStruct((2 * ROWS, NP * 64), jnp.bfloat16)
    partial, panel_both, own_high, own_low = pl.pallas_call(
        own_kernel,
        out_shape=(
            jax.ShapeDtypeStruct((ROWS, S1), jnp.float32),
            panel_shape,
            lower_shape,
            lower_shape,
        ),
        in_specs=in_vmem(4),
        out_specs=tuple(in_vmem(4)),
        scratch_shapes=[
            pltpu.VMEM((ROWS, NP * BLK), jnp.float32),
            pltpu.VMEM((2 * ROWS, NP * 64), jnp.bfloat16),
        ],
        compiler_params=params,
    )(chosen, *near_parts, far)
    cross, pieces, other_high, other_low = pl.pallas_call(
        cross_kernel,
        out_shape=(
            jax.ShapeDtypeStruct((1, ROWS, S1), jnp.float32),
            jax.ShapeDtypeStruct((N_GRID * PIECE3, BLK), jnp.float32),
            lower_shape,
            lower_shape,
        ),
        in_specs=in_vmem(5),
        out_specs=tuple(in_vmem(4)),
        scratch_shapes=[pltpu.VMEM((ROWS, S1), jnp.float32)],
        compiler_params=params,
    )(partial, panel_both, *near_other, far_other)
    pieces = lax.all_to_all(
        pieces.reshape(N_GRID, PIECE3, 1, BLK), GRID, 0, 0, tiled=True
    ).reshape(N_GRID * PIECE3, BLK)
    diagonal = pl.pallas_call(
        diagonal_kernel,
        out_shape=jax.ShapeDtypeStruct((COLS, 1, S1), jnp.float32),
        in_specs=[pl.BlockSpec(memory_space=pltpu.SMEM)] + in_vmem(6),
        out_specs=in_vmem(1)[0],
        scratch_shapes=[pltpu.VMEM((NP, 32, BLK), jnp.float32)]
        + [pltpu.VMEM((64, NP * 64), jnp.bfloat16)] * 2,
        compiler_params=params,
    )(
        pattern,
        pieces,
        own_high,
        own_low,
        other_high,
        other_low,
        jnp.transpose(child_diag_inv, (1, 0, 2)),
    )
    return cross, jnp.transpose(diagonal, (1, 0, 2))


def solution(mesh):
    shape = mesh.shape
    parts = Mesh(
        mesh.devices.reshape(shape["leaf"], shape["prow"], shape["pcol"] // 2, 2), ("leaf",) + GRID
    )
    return jax.shard_map(
        shards,
        mesh=parts,
        in_specs=(
            P(GRID, "leaf"),
            P("leaf", None),
            P("leaf", GRID, None),
            P("leaf", GRID, None),
        ),
        out_specs=(P("leaf", GRID, None), P("leaf", GRID, None)),
        check_vma=False,
    )
```
